512 devices in a mesh: shard: 128 (over z_hi, x, y), tp: 4 (over z_lo, core).
Axes of the slice: x: 4, y: 8, z: 8 (z_hi: 4, z_lo: 2; z = z_hi * 2 + z_lo), core: 2. Of those that a mesh axis runs over, the one named last changes fastest.
Arguments:
- features: bfloat16 [32768, 2048], P('shard', 'tp'), may hold values from -50 to 50, as said below
- item_id: int32 [32768], P('shard'), may hold values from 0 to 262143, as said below
- w_in: bfloat16 [2048, 4096], P('shard', 'tp'), may hold values from -0.125 to 0.125
- bias_in: float32 [4096], P('tp'), may hold values from -3 to 3
- w_out: bfloat16 [1024, 4096], P('shard', 'tp'), may hold values from -16 to 16
- bias_out: float32 [1024], replicated, may hold values from -4 to 4
- item_table: bfloat16 [262144, 1024], P('shard', 'tp'), may hold values from -4 to 4
Outputs:
- new_table: bfloat16 [262144, 1024], P('shard', 'tp')
The draws below stay inside these ranges and needn't reach their ends.
Inputs may be any that keep to these rules, and one draw needn't show every extreme that they name: `features`: feature rows of order one to sixteen. All ids differ. With owner = item_id // 2048, the 256 items of one index of shard (an aligned block) name one owner at most 4 times, and some owner is named exactly 4 times by every block.
All inputs are finite; a program needn't handle non-finite values.
Results may differ from the reference program's by a relative error of at most 0.0029.
Values may be sent and summed in bfloat16 or wider, within the bound.
No kernel may reach another device: no remote copies, remote signals or barrier semaphores. Data moves between devices by JAX's collectives and lax.ppermute only.
A program may use at most 64 MiB of HBM per device.

```python
import jax
import jax.numpy as jnp
from jax import lax

D_IN = 2048
D_HID = 4096
D_OUT = 1024
SRC_ROWS = 256
OWN_ROWS = 2048
OWNERS = 128
CAP = 4
ITEMS = 32768
TABLE_ROWS = 262144


def draw_features(key, part):
    key = jax.random.fold_in(key, 11)
    key_base, key_scale = jax.random.split(key)
    spread = jax.random.uniform(key_scale, (ITEMS, 1), jnp.float32)
    base = jnp.clip(jax.random.normal(key_base, (ITEMS, D_IN), jnp.float32), -5.0, 5.0)
    row_scale = 10.0 ** spread
    return (base * row_scale).astype(jnp.bfloat16)


def draw_w_out(key, part):
    key = jax.random.fold_in(key, 12)
    key_base, key_scale = jax.random.split(key, 2)
    spread = jax.random.uniform(key_scale, (D_OUT, 1), jnp.float32)
    ramp = jnp.arange(D_OUT, dtype=jnp.float32)[:, None] / (D_OUT - 1)
    base = jnp.clip(jax.random.normal(key_base, (D_OUT, D_HID), jnp.float32), -5.0, 5.0)
    row_scale = 10.0 ** spread
    values = base * row_scale * 3.0 ** (0.5 * ramp) * D_HID ** (-0.5)
    return values.astype(jnp.bfloat16)


def draw_item_id(key, part):
    key = jax.random.fold_in(key, 13)
    key_pop, key_hot, key_src, key_rows = jax.random.split(key, 4)
    popular = jax.random.randint(key_pop, (OWNERS,), 1, 9)
    hottest = jax.random.randint(key_hot, (), 0, OWNERS)
    owner_ids = jnp.arange(OWNERS, dtype=jnp.int32)
    slot_pos = jnp.arange(CAP, dtype=jnp.int32)
    tier = slot_pos[None, :] * 64 // popular[:, None]
    tier = jnp.where(owner_ids[:, None] == hottest, -1, tier)
    edge_owner = (owner_ids[:, None] == 0) | (owner_ids[:, None] == OWNERS - 1)
    tier = jnp.where(edge_owner & (slot_pos[None, :] == 0), -1, tier)

    def one_source(source_key):
        key_noise, key_perm = jax.random.split(source_key)
        noise = jax.random.randint(key_noise, (OWNERS, CAP), 0, 2048)
        score = (tier * 2048 + noise).reshape(-1)
        chosen = jnp.argsort(score, stable=True)[:SRC_ROWS]
        return jax.random.permutation(key_perm, chosen // CAP)
    owners = jax.vmap(one_source)(jax.random.split(key_src, OWNERS)).reshape(-1).astype(jnp.int32)
    matches = (owners[:, None] == owner_ids[None, :]).astype(jnp.int32)
    ranks = jnp.sum((jnp.cumsum(matches, axis=0) - 1) * matches, axis=1)
    perms = jax.vmap(lambda each: jax.random.permutation(each, OWN_ROWS))(jax.random.split(key_rows, OWNERS)).astype(jnp.int32)
    offsets = jnp.where(owner_ids == 0, 0, -1)
    perms = (perms - perms[:, :1] + offsets[:, None]) % OWN_ROWS
    rows = perms[owners, ranks]
    return (owners * OWN_ROWS + rows).astype(jnp.int32)


def steps_of(key, extent, pieces, smallest, high):
    def one(position, shards_of):
        steps = jax.random.uniform(jax.random.fold_in(jax.random.fold_in(key, 6), position), (shards_of,), jnp.float32, smallest / len(pieces), high / len(pieces))
        return jnp.repeat(jnp.exp(steps), extent[position] // shards_of).reshape((-1,) + (1,) * (len(extent) - position - 1))

    level = one(*pieces[0])
    for cut in pieces[1:]:
        level = level * one(*cut)
    return level


def gaussian(key, dims, deviation, most, cuts=(), kind=jnp.bfloat16):
    drawn = jax.random.normal(key, dims, jnp.float32) * deviation
    if len(cuts) > 0:
        drawn = steps_of(key, dims, cuts, -0.22, 0.18) * drawn
    return jnp.clip(drawn, min=-most, max=most).astype(kind)


def setup_inputs(seed: int = 0) -> dict:
    key_of = jax.random.split(jax.random.key(seed), 8)
    return {
        "features": draw_features(jax.random.fold_in(key_of[7], 71), 0),
        "item_id": draw_item_id(jax.random.fold_in(key_of[7], 71), 0),
        "w_in": gaussian(key_of[2], (D_IN, D_HID), D_IN ** -0.5, 0.125, ((0, 128), (1, 4))),
        "bias_in": gaussian(key_of[3], (D_HID,), 0.5, 3.0, ((0, 4),), jnp.float32),
        "w_out": draw_w_out(jax.random.fold_in(key_of[7], 71), 0),
        "bias_out": gaussian(key_of[5], (D_OUT,), 1.0, 4.0, (), jnp.float32),
        "item_table": gaussian(key_of[6], (TABLE_ROWS, D_OUT), 1.0, 4.0, ((0, 128), (1, 4))),
    }


def reference(features, item_id, w_in, bias_in, w_out, bias_out, item_table):
    blocks = features.reshape(OWNERS, SRC_ROWS, D_IN)

    def embed(block):
        activation = jnp.dot(block, w_in, preferred_element_type=jnp.float32) + bias_in
        hidden = jax.nn.silu(activation).astype(jnp.bfloat16)
        projected = jnp.dot(hidden, w_out.T, preferred_element_type=jnp.float32) + bias_out
        scaled = projected * lax.rsqrt(lax.optimization_barrier(jnp.mean(projected * projected, axis=1, keepdims=True)) + 1e-06)
        return scaled.astype(jnp.bfloat16)
    embedding = lax.map(embed, blocks).reshape(ITEMS, D_OUT)
    return item_table.at[item_id].set(embedding)
```

```python
import jax
import jax.numpy as jnp
from jax import lax
from jax.experimental import pallas as pl
from jax.experimental.pallas import tpu as pltpu
from jax.sharding import Mesh, PartitionSpec as P

AXES = ("zh", "x", "yh", "yl", "zl", "core")
SIZES = (4, 4, 4, 2, 2, 2)
SHARD = ("zh", "x", "yh", "yl")
TP = ("zl", "core")
GROUP = ("yl", "zl", "core")
PLANE = ("zh", "yh", "yl")

SRC = 256
CAP = 4
OWNERS = 128
OWN_ROWS = 2048
D_OUT = 1024
SHARE = 256
HID = 512
META = 128
ORDER = (0, 3, 1, 2)
BF16 = jnp.bfloat16
F32 = jnp.float32


def tower_kernel(x_ref, feat_ref, w_in_ref, w_out_ref, bias_ref, out_ref, w_all):
    x0 = x_ref[0]
    act = [None, None]
    for k, offset in enumerate(ORDER):
        xk = lax.rem(x0 + offset, 4)
        col = pl.multiple_of(xk * 128, 128)
        weights = w_in_ref[k].reshape(4 * 128, HID)
        for half in range(2):
            columns = jnp.concatenate(
                [feat_ref[half * 4 + zh, :, pl.ds(col, 128)] for zh in range(4)], axis=1
            )
            term = jnp.dot(columns, weights, preferred_element_type=F32)
            act[half] = term if act[half] is None else act[half] + term
        for zh in range(4):
            row = pl.multiple_of(zh * 256 + xk * 64, 64)
            w_all[pl.ds(row, 64), :] = w_out_ref[k, zh]
    for half in range(2):
        v = act[half] + bias_ref[...]
        hidden = (v * (1.0 / (1.0 + jnp.exp(-v)))).astype(BF16)
        part = lax.dot_general(
            hidden, w_all[...], (((1,), (1,)), ((), ())), preferred_element_type=F32
        )
        out_ref[half * SRC : (half + 1) * SRC, :] = part.astype(BF16)


def tower(x0, feats, w_in, w_out, bias):
    vmem = pl.BlockSpec(memory_space=pltpu.VMEM)
    return pl.pallas_call(
        tower_kernel,
        out_shape=jax.ShapeDtypeStruct((2 * SRC, D_OUT), BF16),
        in_specs=[pl.BlockSpec(memory_space=pltpu.SMEM), vmem, vmem, vmem, vmem],
        out_specs=vmem,
        scratch_shapes=[pltpu.VMEM((D_OUT, HID), BF16)],
        compiler_params=pltpu.CompilerParams(vmem_limit_bytes=48 << 20),
        name="tower",
    )(x0, feats, w_in, w_out, bias)


def write_kernel(table_ref, rows_ref, out_ref):
    block = table_ref.shape[0]
    first = pl.program_id(0) * block
    meta = rows_ref[:, SHARE:].astype(F32)
    target = (meta[:, 0:1] * 64.0 + meta[:, 1:2]).astype(jnp.int32)
    target = jnp.where(meta[:, 2:3] > 0.5, target - first, -1)
    here = lax.broadcasted_iota(jnp.int32, (rows_ref.shape[0], block), 1) == target
    moved = lax.dot_general(
        here.astype(F32).astype(BF16),
        rows_ref[...],
        (((0,), (0,)), ((), ())),
        preferred_element_type=F32,
    )
    hit = moved[:, SHARE + 2 : SHARE + 3] > 0.5
    out_ref[...] = jnp.where(hit, moved[:, :SHARE], table_ref[...].astype(F32)).astype(BF16)


def write(table, rows):
    block = 256
    spec = pl.BlockSpec((block, SHARE), lambda i: (i, 0))
    return pl.pallas_call(
        write_kernel,
        out_shape=jax.ShapeDtypeStruct(table.shape, BF16),
        grid=(table.shape[0] // block,),
        in_specs=[spec, pl.BlockSpec(rows.shape, lambda i: (0, 0))],
        out_specs=spec,
        compiler_params=pltpu.CompilerParams(vmem_limit_bytes=32 << 20),
        name="write",
    )(table, rows)


def along_x(block, step):
    return lax.ppermute(block, "x", [(i, (i + step) % 4) for i in range(4)])


def local(features, item_id, w_in, bias_in, w_out, bias_out, item_table):
    x0 = lax.axis_index("x").astype(jnp.int32)
    yl = lax.axis_index("yl").astype(jnp.int32)

    feats = lax.all_gather(features, GROUP, axis=0, tiled=True).reshape(8, SRC, 512)

    w = jnp.concatenate([w_in, w_out], axis=0).reshape(24, 2, HID).transpose(1, 0, 2)
    w = jnp.broadcast_to(w[None], (16, 2, 24, HID)).reshape(32, 24, HID)
    mine = lax.all_to_all(w, PLANE, split_axis=0, concat_axis=0, tiled=True)
    left = along_x(mine, 1)
    right = along_x(mine, -1)
    far_a = along_x(left[:16], 1)
    far_b = along_x(right[16:], -1)
    held = jnp.concatenate([mine, left, right, far_a, far_b], axis=0).reshape(4, 32, 24, HID)
    all_in = held[:, :, :16].reshape(4, 4, 128, HID)
    all_out = held[:, :, 16:].reshape(4, 4, 64, HID)
    bias = lax.dynamic_slice_in_dim(bias_in, yl * HID, HID).reshape(1, HID)

    partial = tower(x0.reshape(1), feats, all_in, all_out, bias)
    parts = lax.all_to_all(
        partial.reshape(8, 64, D_OUT), GROUP, split_axis=0, concat_axis=0, tiled=True
    )
    projected = jnp.sum(parts.astype(F32), axis=0) + bias_out
    scale = lax.rsqrt(jnp.mean(projected * projected, axis=1, keepdims=True) + 1e-06)
    embedded = (projected * scale).astype(BF16)
    columns = embedded.reshape(64, 4, SHARE).transpose(1, 0, 2)
    columns = lax.all_to_all(columns, TP, split_axis=0, concat_axis=0, tiled=True)
    columns = columns.reshape(SRC, SHARE)

    owner = item_id // OWN_ROWS
    row = item_id - owner * OWN_ROWS
    order = jnp.arange(SRC, dtype=jnp.int32)
    before = (owner[:, None] == owner[None, :]) & (order[None, :] < order[:, None])
    slot = owner * CAP + jnp.sum(before.astype(jnp.int32), axis=1)
    pick = (jnp.arange(OWNERS * CAP, dtype=jnp.int32)[:, None] == slot[None, :]).astype(BF16)
    lane = jnp.arange(META, dtype=jnp.int32)[None, :]
    meta = jnp.where(
        lane == 0,
        (row >> 6)[:, None],
        jnp.where(lane == 1, (row & 63)[:, None], (lane == 2).astype(jnp.int32)),
    ).astype(BF16)
    payload = jnp.concatenate([columns, meta], axis=1)
    packed = jnp.dot(pick, payload, preferred_element_type=F32).astype(BF16)
    arrived = lax.all_to_all(
        packed.reshape(OWNERS, CAP, SHARE + META), SHARD, split_axis=0, concat_axis=0, tiled=True
    )
    return write(item_table, arrived.reshape(OWNERS * CAP, SHARE + META))


def solution(mesh):
    cut = Mesh(mesh.devices.reshape(SIZES), AXES)
    in_specs = (
        P(SHARD, TP),
        P(SHARD),
        P(SHARD, TP),
        P(TP),
        P(SHARD, TP),
        P(),
        P(SHARD, TP),
    )
    return jax.shard_map(
        local, mesh=cut, in_specs=in_specs, out_specs=P(SHARD, TP), check_vma=False
    )
```

```python
import jax
import jax.numpy as jnp
from jax import lax
from jax.experimental import pallas as pl
from jax.experimental.pallas import tpu as pltpu
from jax.sharding import Mesh, PartitionSpec as P

AXES = ("zh", "x", "yh", "yl", "zl", "core")
SIZES = (4, 4, 4, 2, 2, 2)
SHARD = ("zh", "x", "yh", "yl")
TP = ("zl", "core")
PLANE = ("yh", "zh", "yl")

SRC = 256
CAP = 4
OWNERS = 128
OWN_ROWS = 2048
D_OUT = 1024
SHARE = 256
HID = 512
META = 128
BF16 = jnp.bfloat16
F32 = jnp.float32
VMEM = pl.BlockSpec(memory_space=pltpu.VMEM)
SMEM = pl.BlockSpec(memory_space=pltpu.SMEM)


def tower_kernel(
    place_ref, f0, f1, f2, f3, mine, la, lb, ra, rb, fa, fb, bias_ref, give_ref, keep_ref, w_all, hid
):
    x0, tp, yl, core = (place_ref[i] for i in range(4))
    feats = (f0, f1, f2, f3)
    blocks = (
        (0, mine.at[0:2], mine.at[2:4]),
        (3, la, lb),
        (1, ra, rb),
        (2, fa, fb),
    )
    act = [None, None]
    for offset, first, second in blocks:
        xk = lax.rem(x0 + offset, 4)
        col = pl.multiple_of(xk * 128, 128)
        for pair in ((0, 1), (2, 3)):
            weights = jnp.concatenate(
                [
                    half[:, jnp.bitwise_xor(tp, d), :, 0:16, :].reshape(64, HID)
                    for d in pair
                    for half in (first, second)
                ],
                axis=0,
            )
            for dy in range(2):
                columns = jnp.concatenate(
                    [feats[d][dy, :, pl.ds(col, 128)] for d in pair], axis=1
                )
                term = jnp.dot(columns, weights, preferred_element_type=F32)
                act[dy] = term if act[dy] is None else act[dy] + term
        for zh in range(4):
            rows = jnp.concatenate(
                [half[:, zh].astype(F32)[:, :, 16:24, :].reshape(32, HID) for half in (first, second)],
                axis=0,
            )
            row = pl.multiple_of(zh * 256 + xk * 64, 64)
            w_all[pl.ds(row, 64), :] = rows.astype(BF16)
    for dy in range(2):
        v = act[dy] + bias_ref[...]
        hid[dy] = (v * (1.0 / (1.0 + jnp.exp(-v)))).astype(BF16)
    for out_ref, c in ((give_ref, 1 - core), (keep_ref, core)):
        chunks = [
            hid[dy, pl.ds(pl.multiple_of(zl * 128 + c * 64, 64), 64), :]
            for dy in range(2)
            for zl in range(2)
        ]
        part = lax.dot_general(
            jnp.concatenate(chunks, axis=0),
            w_all[...],
            (((1,), (1,)), ((), ())),
            preferred_element_type=F32,
        ).astype(BF16)
        for dy in range(2):
            for zl in range(2):
                i = dy * 2 + zl
                out_ref[jnp.bitwise_xor(yl, dy) * 2 + zl] = part[i * 64 : (i + 1) * 64]


def tower(place, feats, weights, bias):
    part = jax.ShapeDtypeStruct((4, 64, D_OUT), BF16)
    return pl.pallas_call(
        tower_kernel,
        out_shape=(part, part),
        in_specs=[SMEM] + [VMEM] * 12,
        out_specs=(VMEM, VMEM),
        scratch_shapes=[pltpu.VMEM((D_OUT, HID), BF16), pltpu.VMEM((2, SRC, HID), BF16)],
        compiler_params=pltpu.CompilerParams(vmem_limit_bytes=48 << 20),
        name="tower",
    )(place, *feats, *weights, bias)


def norm_kernel(parts_ref, bias_ref, out_ref):
    projected = bias_ref[...]
    for i in range(4):
        projected = projected + parts_ref[i].astype(F32)
    scale = lax.rsqrt(jnp.mean(projected * projected, axis=1, keepdims=True) + 1e-06)
    scaled = (projected * scale).astype(BF16)
    for q in range(4):
        out_ref[q] = scaled[:, q * SHARE : (q + 1) * SHARE]


def norm(parts, bias):
    return pl.pallas_call(
        norm_kernel,
        out_shape=jax.ShapeDtypeStruct((4, 64, SHARE), BF16),
        in_specs=[VMEM, VMEM],
        out_specs=VMEM,
        compiler_params=pltpu.CompilerParams(vmem_limit_bytes=16 << 20),
        name="norm",
    )(parts, bias)


def write_kernel(table_ref, rows_ref, out_ref, target_ref):
    block = table_ref.shape[0]

    @pl.when(pl.program_id(0) == 0)
    def _():
        lane = lax.broadcasted_iota(jnp.int32, (8, META), 1)
        weight = jnp.where(lane == 0, 64.0, jnp.where(lane == 1, 1.0, 0.0)).astype(BF16)
        target_ref[...] = lax.dot_general(
            weight, rows_ref[:, SHARE:], (((1,), (1,)), ((), ())), preferred_element_type=F32
        )

    row = lax.broadcasted_iota(jnp.int32, (block, 1), 0) + (pl.program_id(0) * block + 1)
    here = row.astype(F32) == target_ref[0:1, :]
    moved = jnp.dot(
        jnp.where(here, 1.0, 0.0).astype(BF16), rows_ref[...], preferred_element_type=F32
    )
    hit = moved[:, SHARE + 2 : SHARE + 3] > 0.5
    out_ref[...] = jnp.where(hit, moved[:, :SHARE], table_ref[...].astype(F32)).astype(BF16)


def write(table, rows):
    block = 256
    spec = pl.BlockSpec((block, SHARE), lambda i: (i, 0))
    return pl.pallas_call(
        write_kernel,
        out_shape=jax.ShapeDtypeStruct(table.shape, BF16),
        grid=(table.shape[0] // block,),
        in_specs=[spec, pl.BlockSpec(rows.shape, lambda i: (0, 0))],
        out_specs=spec,
        scratch_shapes=[pltpu.VMEM((8, rows.shape[0]), F32)],
        compiler_params=pltpu.CompilerParams(vmem_limit_bytes=32 << 20),
        name="write",
    )(table, rows)


def along_x(block, step):
    return lax.ppermute(block, "x", [(i, (i + step) % 4) for i in range(4)])


def swap(block, axis):
    return lax.ppermute(block, axis, [(0, 1), (1, 0)])


def local(features, item_id, w_in, bias_in, w_out, bias_out, item_table):
    index = {axis: lax.axis_index(axis).astype(jnp.int32) for axis in AXES}
    place = jnp.stack([index["x"], index["zl"] * 2 + index["core"], index["yl"], index["core"]])

    both = jnp.stack([features, swap(features, "yl")])
    over = swap(both, "zl")
    feats = (both, swap(both, "core"), over, swap(over, "core"))

    w = jnp.concatenate([w_in, w_out], axis=0).reshape(24, 2, HID).transpose(1, 0, 2)
    w = jnp.broadcast_to(w[None], (16, 2, 24, HID)).reshape(32, 24, HID)
    mine = lax.all_to_all(w, PLANE, split_axis=0, concat_axis=0, tiled=True)
    la, rb = along_x(mine[:16], 1), along_x(mine[16:], -1)
    lb, ra = along_x(mine[16:], 1), along_x(mine[:16], -1)
    fa, fb = along_x(la, 1), along_x(rb, -1)
    halves = [each.reshape(2, 4, 2, 24, HID) for each in (la, lb, ra, rb, fa, fb)]
    weights = [mine.reshape(4, 4, 2, 24, HID)] + halves
    bias = lax.dynamic_slice_in_dim(bias_in, index["yl"] * HID, HID).reshape(1, HID)

    give, keep = tower(place, feats, weights, bias)
    chip = (keep.astype(F32) + swap(give, "core").astype(F32)).astype(BF16)
    parts = lax.all_to_all(chip, ("yl", "zl"), split_axis=0, concat_axis=0, tiled=True)
    columns = norm(parts, bias_out.reshape(1, D_OUT))
    columns = lax.all_to_all(columns, TP, split_axis=0, concat_axis=0, tiled=True)
    columns = columns.reshape(SRC, SHARE)

    owner = item_id // OWN_ROWS
    row = item_id - owner * OWN_ROWS + 1
    order = jnp.arange(SRC, dtype=jnp.int32)
    before = (owner[:, None] == owner[None, :]) & (order[None, :] < order[:, None])
    slot = owner * CAP + jnp.sum(before.astype(jnp.int32), axis=1)
    pick = (jnp.arange(OWNERS * CAP, dtype=jnp.int32)[:, None] == slot[None, :]).astype(BF16)
    lane = jnp.arange(META, dtype=jnp.int32)[None, :]
    meta = jnp.where(
        lane == 0,
        (row >> 6)[:, None],
        jnp.where(lane == 1, (row & 63)[:, None], (lane == 2).astype(jnp.int32)),
    ).astype(BF16)
    payload = jnp.concatenate([columns, meta], axis=1)
    packed = jnp.dot(pick, payload, preferred_element_type=F32).astype(BF16)
    arrived = lax.all_to_all(
        packed.reshape(OWNERS, CAP, SHARE + META), SHARD, split_axis=0, concat_axis=0, tiled=True
    )
    return write(item_table, arrived.reshape(OWNERS * CAP, SHARE + META))


def solution(mesh):
    cut = Mesh(mesh.devices.reshape(SIZES), AXES)
    in_specs = (
        P(SHARD, TP),
        P(SHARD),
        P(SHARD, TP),
        P(TP),
        P(SHARD, TP),
        P(),
        P(SHARD, TP),
    )
    return jax.shard_map(
        local, mesh=cut, in_specs=in_specs, out_specs=P(SHARD, TP), check_vma=False
    )
```

```python
import jax
import jax.numpy as jnp
from jax import lax
from jax.experimental import pallas as pl
from jax.experimental.pallas import tpu as pltpu
from jax.sharding import Mesh, PartitionSpec as P

AXES = ("zh", "x", "yh", "yl", "zl", "core")
SIZES = (4, 4, 4, 2, 2, 2)
SHARD = ("zh", "x", "yh", "yl")
TP = ("zl", "core")
PLANE = ("yh", "zh", "yl")

SRC = 256
CAP = 4
OWNERS = 128
OWN_ROWS = 2048
D_OUT = 1024
SHARE = 256
HID = 512
META = 128
BF16 = jnp.bfloat16
F32 = jnp.float32
VMEM = pl.BlockSpec(memory_space=pltpu.VMEM)
SMEM = pl.BlockSpec(memory_space=pltpu.SMEM)


def pieces_kernel(w_in_ref, w_out_ref, out_ref):
    for yl in range(2):
        cut = pl.ds(yl * HID, HID)
        rows = jnp.concatenate([w_in_ref[:, cut].astype(F32), w_out_ref[:, cut].astype(F32)], axis=0)
        for i in range(16):
            out_ref[i * 2 + yl] = rows.astype(BF16)


def pieces(w_in, w_out):
    return pl.pallas_call(
        pieces_kernel,
        out_shape=jax.ShapeDtypeStruct((32, 24, HID), BF16),
        in_specs=[VMEM, VMEM],
        out_specs=VMEM,
        cost_estimate=pl.CostEstimate(flops=0, bytes_accessed=64 << 20, transcendentals=0),
        compiler_params=pltpu.CompilerParams(vmem_limit_bytes=16 << 20),
        name="pieces",
    )(w_in, w_out)


def tower_kernel(
    place_ref, near, far, mine, la, lb, ra, rb, fa, fb, bias_ref, give_ref, keep_ref, w_all, hid
):
    x0, tp, yl, core = (place_ref[i] for i in range(4))
    feats = (near, far)
    blocks = (
        (0, mine.at[0:2], mine.at[2:4]),
        (3, la, lb),
        (1, ra, rb),
        (2, fa, fb),
    )
    act = [None, None]
    for offset, first, second in blocks:
        xk = lax.rem(x0 + offset, 4)
        col = pl.multiple_of(xk * 128, 128)
        for dz in range(2):
            weights = jnp.concatenate(
                [
                    half[:, jnp.bitwise_xor(tp, dz * 2 + dc), :, 0:16, :].reshape(64, HID)
                    for dc in range(2)
                    for half in (first, second)
                ],
                axis=0,
            )
            for dy in range(2):
                columns = jnp.concatenate(
                    [feats[dz][dy, dc, :, pl.ds(col, 128)] for dc in range(2)], axis=1
                )
                term = jnp.dot(columns, weights, preferred_element_type=F32)
                act[dy] = term if act[dy] is None else act[dy] + term
        for zh in range(4):
            rows = jnp.concatenate(
                [half[:, zh].astype(F32)[:, :, 16:24, :].reshape(32, HID) for half in (first, second)],
                axis=0,
            )
            row = pl.multiple_of(zh * 256 + xk * 64, 64)
            w_all[pl.ds(row, 64), :] = rows.astype(BF16)
    for dy in range(2):
        v = act[dy] + bias_ref[...]
        hid[dy] = (v * (1.0 / (1.0 + jnp.exp(-v)))).astype(BF16)
    for out_ref, c in ((give_ref, 1 - core), (keep_ref, core)):
        chunks = [
            hid[dy, pl.ds(pl.multiple_of(zl * 128 + c * 64, 64), 64), :]
            for dy in range(2)
            for zl in range(2)
        ]
        part = lax.dot_general(
            jnp.concatenate(chunks, axis=0),
            w_all[...],
            (((1,), (1,)), ((), ())),
            preferred_element_type=F32,
        ).astype(BF16)
        for dy in range(2):
            for zl in range(2):
                i = dy * 2 + zl
                out_ref[jnp.bitwise_xor(yl, dy) * 2 + zl] = part[i * 64 : (i + 1) * 64]


def tower(place, feats, weights, bias):
    part = jax.ShapeDtypeStruct((4, 64, D_OUT), BF16)
    return pl.pallas_call(
        tower_kernel,
        out_shape=(part, part),
        in_specs=[SMEM] + [VMEM] * 10,
        out_specs=(VMEM, VMEM),
        scratch_shapes=[pltpu.VMEM((D_OUT, HID), BF16), pltpu.VMEM((2, SRC, HID), BF16)],
        compiler_params=pltpu.CompilerParams(vmem_limit_bytes=48 << 20),
        name="tower",
    )(place, *feats, *weights, bias)


def norm_kernel(parts_ref, bias_ref, out_ref):
    projected = bias_ref[...]
    for i in range(4):
        projected = projected + parts_ref[i].astype(F32)
    scale = lax.rsqrt(jnp.mean(projected * projected, axis=1, keepdims=True) + 1e-06)
    scaled = (projected * scale).astype(BF16)
    for q in range(4):
        out_ref[q] = scaled[:, q * SHARE : (q + 1) * SHARE]


def norm(parts, bias):
    return pl.pallas_call(
        norm_kernel,
        out_shape=jax.ShapeDtypeStruct((4, 64, SHARE), BF16),
        in_specs=[VMEM, VMEM],
        out_specs=VMEM,
        compiler_params=pltpu.CompilerParams(vmem_limit_bytes=16 << 20),
        name="norm",
    )(parts, bias)


def write_kernel(table_ref, rows_ref, out_ref, target_ref):
    block = table_ref.shape[0]

    @pl.when(pl.program_id(0) == 0)
    def _():
        lane = lax.broadcasted_iota(jnp.int32, (8, META), 1)
        weight = jnp.where(lane == 0, 64.0, jnp.where(lane == 1, 1.0, 0.0)).astype(BF16)
        target_ref[...] = lax.dot_general(
            weight, rows_ref[:, SHARE:], (((1,), (1,)), ((), ())), preferred_element_type=F32
        )

    row = lax.broadcasted_iota(jnp.int32, (block, 1), 0) + (pl.program_id(0) * block + 1)
    here = jnp.where(row.astype(F32) == target_ref[0:1, :], 1.0, 0.0)
    moved = jnp.dot(here.astype(BF16), rows_ref[:, :SHARE], preferred_element_type=F32)
    hit = jnp.max(here, axis=1, keepdims=True) > 0.5
    out_ref[...] = jnp.where(hit, moved, table_ref[...].astype(F32)).astype(BF16)


def write(table, rows):
    block = 512
    spec = pl.BlockSpec((block, SHARE), lambda i: (i, 0))
    return pl.pallas_call(
        write_kernel,
        out_shape=jax.ShapeDtypeStruct(table.shape, BF16),
        grid=(table.shape[0] // block,),
        in_specs=[spec, pl.BlockSpec(rows.shape, lambda i: (0, 0))],
        out_specs=spec,
        scratch_shapes=[pltpu.VMEM((8, rows.shape[0]), F32)],
        compiler_params=pltpu.CompilerParams(vmem_limit_bytes=32 << 20),
        name="write",
    )(table, rows)


def along_x(block, step):
    return lax.ppermute(block, "x", [(i, (i + step) % 4) for i in range(4)])


def swap(block, axis):
    return lax.ppermute(block, axis, [(0, 1), (1, 0)])


def local(features, item_id, w_in, bias_in, w_out, bias_out, item_table):
    index = {axis: lax.axis_index(axis).astype(jnp.int32) for axis in AXES}
    place = jnp.stack([index["x"], index["zl"] * 2 + index["core"], index["yl"], index["core"]])

    w = pieces(w_in, w_out)
    mine = lax.all_to_all(w, PLANE, split_axis=0, concat_axis=0, tiled=True)
    pair = jnp.stack([features, swap(features, "core")])
    mine, near = lax.optimization_barrier((mine, swap(pair, "yl")))
    la, rb = along_x(mine[:16], 1), along_x(mine[16:], -1)
    lb, ra = along_x(mine[16:], 1), along_x(mine[:16], -1)
    fa, fb = along_x(la, 1), along_x(rb, -1)

    near = jnp.stack([pair, near])
    feats = (near, swap(near, "zl"))

    halves = [each.reshape(2, 4, 2, 24, HID) for each in (la, lb, ra, rb, fa, fb)]
    weights = [mine.reshape(4, 4, 2, 24, HID)] + halves
    bias = lax.dynamic_slice_in_dim(bias_in, index["yl"] * HID, HID).reshape(1, HID)

    give, keep = tower(place, feats, weights, bias)
    chip = (keep.astype(F32) + swap(give, "core").astype(F32)).astype(BF16)
    parts = lax.all_to_all(chip, ("yl", "zl"), split_axis=0, concat_axis=0, tiled=True)
    columns = norm(parts, bias_out.reshape(1, D_OUT))
    columns = lax.all_to_all(columns, TP, split_axis=0, concat_axis=0, tiled=True)
    columns = columns.reshape(SRC, SHARE)

    owner = item_id // OWN_ROWS
    row = item_id - owner * OWN_ROWS + 1
    order = jnp.arange(SRC, dtype=jnp.int32)
    before = (owner[:, None] == owner[None, :]) & (order[None, :] < order[:, None])
    slot = owner * CAP + jnp.sum(before.astype(jnp.int32), axis=1)
    pick = (jnp.arange(OWNERS * CAP, dtype=jnp.int32)[:, None] == slot[None, :]).astype(BF16)
    lane = jnp.arange(META, dtype=jnp.int32)[None, :]
    meta = jnp.where(
        lane == 0,
        (row >> 6)[:, None],
        jnp.where(lane == 1, (row & 63)[:, None], 0),
    ).astype(BF16)
    payload = jnp.concatenate([columns, meta], axis=1)
    packed = jnp.dot(pick, payload, preferred_element_type=F32).astype(BF16)
    arrived = lax.all_to_all(
        packed.reshape(OWNERS, CAP, SHARE + META), SHARD, split_axis=0, concat_axis=0, tiled=True
    )
    return write(item_table, arrived.reshape(OWNERS * CAP, SHARE + META))


def solution(mesh):
    cut = Mesh(mesh.devices.reshape(SIZES), AXES)
    in_specs = (
        P(SHARD, TP),
        P(SHARD),
        P(SHARD, TP),
        P(TP),
        P(SHARD, TP),
        P(),
        P(SHARD, TP),
    )
    return jax.shard_map(
        local, mesh=cut, in_specs=in_specs, out_specs=P(SHARD, TP), check_vma=False
    )
```

```python
import jax
import jax.numpy as jnp
from jax import lax
from jax.experimental import pallas as pl
from jax.experimental.pallas import tpu as pltpu
from jax.sharding import Mesh, PartitionSpec as P

AXES = ("zh", "x", "yh", "yl", "zl", "core")
SIZES = (4, 4, 4, 2, 2, 2)
SHARD = ("zh", "x", "yh", "yl")
TP = ("zl", "core")
PLANE = ("yh", "zh", "yl")

SRC = 256
CAP = 4
OWNERS = 128
OWN_ROWS = 2048
D_OUT = 1024
SHARE = 256
HID = 512
META = 128
BF16 = jnp.bfloat16
F32 = jnp.float32
VMEM = pl.BlockSpec(memory_space=pltpu.VMEM)
SMEM = pl.BlockSpec(memory_space=pltpu.SMEM)


def pieces_kernel(w_in_ref, w_out_ref, out_ref):
    for yl in range(2):
        cut = pl.ds(yl * HID, HID)
        rows = jnp.concatenate([w_in_ref[:, cut].astype(F32), w_out_ref[:, cut].astype(F32)], axis=0)
        for i in range(16):
            out_ref[i * 2 + yl] = rows.astype(BF16)


def pieces(w_in, w_out):
    return pl.pallas_call(
        pieces_kernel,
        out_shape=jax.ShapeDtypeStruct((32, 24, HID), BF16),
        in_specs=[VMEM, VMEM],
        out_specs=VMEM,
        cost_estimate=pl.CostEstimate(flops=0, bytes_accessed=64 << 20, transcendentals=0),
        compiler_params=pltpu.CompilerParams(vmem_limit_bytes=16 << 20),
        name="pieces",
    )(w_in, w_out)


def tower_kernel(
    place_ref, f0, f1, f2, f3, mine, la, lb, ra, rb, fa, fb, bias_ref, give_ref, keep_ref, w_all, hid
):
    x0, tp, yl, core = (place_ref[i] for i in range(4))
    feats = ((f0, f1), (f2, f3))
    blocks = (
        (0, mine.at[0:2], mine.at[2:4]),
        (3, la, lb),
        (1, ra, rb),
        (2, fa, fb),
    )
    act = [None, None]
    for offset, first, second in blocks:
        xk = lax.rem(x0 + offset, 4)
        col = pl.multiple_of(xk * 128, 128)
        for dz in range(2):
            weights = jnp.concatenate(
                [
                    half[:, jnp.bitwise_xor(tp, dz * 2 + dc), :, 0:16, :].reshape(64, HID)
                    for dc in range(2)
                    for half in (first, second)
                ],
                axis=0,
            )
            for dy in range(2):
                columns = jnp.concatenate(
                    [feats[dz][dy][dc, :, pl.ds(col, 128)] for dc in range(2)], axis=1
                )
                term = jnp.dot(columns, weights, preferred_element_type=F32)
                act[dy] = term if act[dy] is None else act[dy] + term
        for zh in range(4):
            rows = jnp.concatenate(
                [half[:, zh].astype(F32)[:, :, 16:24, :].reshape(32, HID) for half in (first, second)],
                axis=0,
            )
            row = pl.multiple_of(zh * 256 + xk * 64, 64)
            w_all[pl.ds(row, 64), :] = rows.astype(BF16)
    for dy in range(2):
        v = act[dy] + bias_ref[...]
        hid[dy] = (v * (1.0 / (1.0 + jnp.exp(-v)))).astype(BF16)
    for out_ref, c in ((give_ref, 1 - core), (keep_ref, core)):
        chunks = [
            hid[dy, pl.ds(pl.multiple_of(zl * 128 + c * 64, 64), 64), :]
            for dy in range(2)
            for zl in range(2)
        ]
        part = lax.dot_general(
            jnp.concatenate(chunks, axis=0),
            w_all[...],
            (((1,), (1,)), ((), ())),
            preferred_element_type=F32,
        ).astype(BF16)
        for dy in range(2):
            for zl in range(2):
                i = dy * 2 + zl
                out_ref[jnp.bitwise_xor(yl, dy) * 2 + zl] = part[i * 64 : (i + 1) * 64]


def tower(place, feats, weights, bias):
    part = jax.ShapeDtypeStruct((4, 64, D_OUT), BF16)
    return pl.pallas_call(
        tower_kernel,
        out_shape=(part, part),
        in_specs=[SMEM] + [VMEM] * 12,
        out_specs=(VMEM, VMEM),
        scratch_shapes=[pltpu.VMEM((D_OUT, HID), BF16), pltpu.VMEM((2, SRC, HID), BF16)],
        compiler_params=pltpu.CompilerParams(vmem_limit_bytes=48 << 20),
        name="tower",
    )(place, *feats, *weights, bias)


def norm_kernel(parts_ref, bias_ref, out_ref):
    projected = bias_ref[...]
    for i in range(4):
        projected = projected + parts_ref[i].astype(F32)
    scale = lax.rsqrt(jnp.mean(projected * projected, axis=1, keepdims=True) + 1e-06)
    scaled = (projected * scale).astype(BF16)
    for q in range(4):
        out_ref[q] = scaled[:, q * SHARE : (q + 1) * SHARE]


def norm(parts, bias):
    return pl.pallas_call(
        norm_kernel,
        out_shape=jax.ShapeDtypeStruct((4, 64, SHARE), BF16),
        in_specs=[VMEM, VMEM],
        out_specs=VMEM,
        compiler_params=pltpu.CompilerParams(vmem_limit_bytes=16 << 20),
        name="norm",
    )(parts, bias)


def write_kernel(table_ref, rows_ref, out_ref, target_ref):
    block = table_ref.shape[0]

    @pl.when(pl.program_id(0) == 0)
    def _():
        lane = lax.broadcasted_iota(jnp.int32, (8, META), 1)
        weight = jnp.where(lane == 0, 64.0, jnp.where(lane == 1, 1.0, 0.0)).astype(BF16)
        target_ref[...] = lax.dot_general(
            weight, rows_ref[:, SHARE:], (((1,), (1,)), ((), ())), preferred_element_type=F32
        )

    row = lax.broadcasted_iota(jnp.int32, (block, 1), 0) + (pl.program_id(0) * block + 1)
    here = jnp.where(row.astype(F32) == target_ref[0:1, :], 1.0, 0.0)
    moved = jnp.dot(here.astype(BF16), rows_ref[:, :SHARE], preferred_element_type=F32)
    hit = jnp.max(here, axis=1, keepdims=True) > 0.5
    out_ref[...] = jnp.where(hit, moved, table_ref[...].astype(F32)).astype(BF16)


def write(table, rows):
    block = 512
    spec = pl.BlockSpec((block, SHARE), lambda i: (i, 0))
    return pl.pallas_call(
        write_kernel,
        out_shape=jax.ShapeDtypeStruct(table.shape, BF16),
        grid=(table.shape[0] // block,),
        in_specs=[spec, pl.BlockSpec(rows.shape, lambda i: (0, 0))],
        out_specs=spec,
        scratch_shapes=[pltpu.VMEM((8, rows.shape[0]), F32)],
        compiler_params=pltpu.CompilerParams(vmem_limit_bytes=32 << 20),
        name="write",
    )(table, rows)


def along_x(block, step):
    return lax.ppermute(block, "x", [(i, (i + step) % 4) for i in range(4)])


def swap(block, axis):
    return lax.ppermute(block, axis, [(0, 1), (1, 0)])


def local(features, item_id, w_in, bias_in, w_out, bias_out, item_table):
    index = {axis: lax.axis_index(axis).astype(jnp.int32) for axis in AXES}
    place = jnp.stack([index["x"], index["zl"] * 2 + index["core"], index["yl"], index["core"]])

    w = pieces(w_in, w_out)
    mine = lax.all_to_all(w, PLANE, split_axis=0, concat_axis=0, tiled=True)
    pair = jnp.stack([features, swap(features, "core")])
    mine, pair = lax.optimization_barrier((mine, pair))
    near = swap(pair, "yl")
    over = swap(pair, "zl")
    la, rb = along_x(mine[:16], 1), along_x(mine[16:], -1)
    lb, ra = along_x(mine[16:], 1), along_x(mine[:16], -1)
    fa, fb = along_x(la, 1), along_x(rb, -1)

    feats = (pair, near, over, swap(near, "zl"))

    halves = [each.reshape(2, 4, 2, 24, HID) for each in (la, lb, ra, rb, fa, fb)]
    weights = [mine.reshape(4, 4, 2, 24, HID)] + halves
    bias = lax.dynamic_slice_in_dim(bias_in, index["yl"] * HID, HID).reshape(1, HID)

    give, keep = tower(place, feats, weights, bias)
    chip = (keep.astype(F32) + swap(give, "core").astype(F32)).astype(BF16)
    parts = lax.all_to_all(chip, ("yl", "zl"), split_axis=0, concat_axis=0, tiled=True)
    columns = norm(parts, bias_out.reshape(1, D_OUT))
    columns = lax.all_to_all(columns, TP, split_axis=0, concat_axis=0, tiled=True)
    columns = columns.reshape(SRC, SHARE)

    owner = item_id // OWN_ROWS
    row = item_id - owner * OWN_ROWS + 1
    order = jnp.arange(SRC, dtype=jnp.int32)
    before = (owner[:, None] == owner[None, :]) & (order[None, :] < order[:, None])
    slot = owner * CAP + jnp.sum(before.astype(jnp.int32), axis=1)
    pick = (jnp.arange(OWNERS * CAP, dtype=jnp.int32)[:, None] == slot[None, :]).astype(BF16)
    lane = jnp.arange(META, dtype=jnp.int32)[None, :]
    meta = jnp.where(
        lane == 0,
        (row >> 6)[:, None],
        jnp.where(lane == 1, (row & 63)[:, None], 0),
    ).astype(BF16)
    payload = jnp.concatenate([columns, meta], axis=1)
    packed = jnp.dot(pick, payload, preferred_element_type=F32).astype(BF16)
    arrived = lax.all_to_all(
        packed.reshape(OWNERS, CAP, SHARE + META), SHARD, split_axis=0, concat_axis=0, tiled=True
    )
    return write(item_table, arrived.reshape(OWNERS * CAP, SHARE + META))


def solution(mesh):
    cut = Mesh(mesh.devices.reshape(SIZES), AXES)
    in_specs = (
        P(SHARD, TP),
        P(SHARD),
        P(SHARD, TP),
        P(TP),
        P(SHARD, TP),
        P(),
        P(SHARD, TP),
    )
    return jax.shard_map(
        local, mesh=cut, in_specs=in_specs, out_specs=P(SHARD, TP), check_vma=False
    )
```

```python
import jax
import jax.numpy as jnp
from jax import lax
from jax.experimental import pallas as pl
from jax.experimental.pallas import tpu as pltpu
from jax.sharding import Mesh, PartitionSpec as P

AXES = ("zh", "x", "yh", "yl", "zl", "core")
SIZES = (4, 4, 4, 2, 2, 2)
SHARD = ("zh", "x", "yh", "yl")
TP = ("zl", "core")
ROUTE = ("yl", "yh", "x", "zh")
PLANE = ("yh", "zh", "yl")

SRC = 256
CAP = 4
OWNERS = 128
OWN_ROWS = 2048
D_OUT = 1024
SHARE = 256
HID = 512
META = 128
BF16 = jnp.bfloat16
F32 = jnp.float32
VMEM = pl.BlockSpec(memory_space=pltpu.VMEM)
SMEM = pl.BlockSpec(memory_space=pltpu.SMEM)


def add_block(x0, tp, offset, first, second, feats, act, w_all):
    xk = lax.rem(x0 + offset, 4)
    col = pl.multiple_of(xk * 128, 128)
    act = list(act)
    for dz in range(2):
        weights = jnp.concatenate(
            [
                half[:, jnp.bitwise_xor(tp, dz * 2 + dc), :, 0:16, :].reshape(64, HID)
                for dc in range(2)
                for half in (first, second)
            ],
            axis=0,
        )
        for dy in range(2):
            columns = jnp.concatenate(
                [feats[dz][dy][dc, :, pl.ds(col, 128)] for dc in range(2)], axis=1
            )
            term = jnp.dot(columns, weights, preferred_element_type=F32)
            act[dy] = term if act[dy] is None else act[dy] + term
    for zh in range(4):
        rows = jnp.concatenate(
            [half[:, zh].astype(F32)[:, :, 16:24, :].reshape(32, HID) for half in (first, second)],
            axis=0,
        )
        row = pl.multiple_of(zh * 256 + xk * 64, 64)
        w_all[pl.ds(row, 64), :] = rows.astype(BF16)
    return act


def early_kernel(place_ref, f0, f1, f2, f3, mine, la, lb, ra, rb, act_ref, w_all):
    x0, tp = place_ref[0], place_ref[1]
    feats = ((f0, f1), (f2, f3))
    act = [None, None]
    for offset, first, second in ((0, mine.at[0:2], mine.at[2:4]), (3, la, lb), (1, ra, rb)):
        act = add_block(x0, tp, offset, first, second, feats, act, w_all)
    for dy in range(2):
        act_ref[dy] = act[dy]


def late_kernel(
    place_ref, f0, f1, f2, f3, fa, fb, bias_ref, act_ref, old_ref, give_ref, kept_ref, w_all, hid
):
    x0, tp, yl, core = (place_ref[i] for i in range(4))
    feats = ((f0, f1), (f2, f3))
    act = add_block(x0, tp, 2, fa, fb, feats, [act_ref[0], act_ref[1]], w_all)
    for dy in range(2):
        v = act[dy] + bias_ref[...]
        hid[dy] = (v * (1.0 / (1.0 + jnp.exp(-v)))).astype(BF16)

    def chunks(c):
        return [
            hid[dy, pl.ds(pl.multiple_of(zl * 128 + c * 64, 64), 64), :]
            for dy in range(2)
            for zl in range(2)
        ]

    part = lax.dot_general(
        jnp.concatenate(chunks(1 - core), axis=0),
        w_all[...],
        (((1,), (1,)), ((), ())),
        preferred_element_type=F32,
    ).astype(BF16)
    for i, chunk in enumerate(chunks(core)):
        slot = (i % 2) * 2 + jnp.bitwise_xor(yl, i // 2)
        give_ref[slot] = part[i * 64 : (i + 1) * 64]
        kept_ref[pl.ds(pl.multiple_of(slot * 64, 64), 64), :] = chunk


def kept_kernel(kept_ref, w_all, out_ref):
    part = lax.dot_general(
        kept_ref[...], w_all[...], (((1,), (1,)), ((), ())), preferred_element_type=F32
    )
    out_ref[...] = part.astype(BF16).reshape(out_ref.shape)


def cost(flops, moved):
    return pl.CostEstimate(flops=flops, bytes_accessed=moved, transcendentals=0)


def tower(place, feats, weights, bias):
    params = pltpu.CompilerParams(vmem_limit_bytes=48 << 20)
    part = jax.ShapeDtypeStruct((4, 64, D_OUT), BF16)
    w_shape = jax.ShapeDtypeStruct((D_OUT, HID), BF16)
    act, w_all = pl.pallas_call(
        early_kernel,
        out_shape=(jax.ShapeDtypeStruct((2, SRC, HID), F32), w_shape),
        in_specs=[SMEM] + [VMEM] * 9,
        out_specs=(VMEM, VMEM),
        compiler_params=params,
        cost_estimate=cost(6 * SRC * 1536 * HID, 6 << 20),
        name="early",
    )(place, *feats, *weights[:5])
    give, kept, w_all = pl.pallas_call(
        late_kernel,
        out_shape=(part, jax.ShapeDtypeStruct((SRC, HID), BF16), w_shape),
        in_specs=[SMEM] + [VMEM] * 9,
        out_specs=(VMEM, VMEM, VMEM),
        scratch_shapes=[pltpu.VMEM((2, SRC, HID), BF16)],
        input_output_aliases={9: 2},
        compiler_params=params,
        cost_estimate=cost(4 * SRC * 1024 * HID, 6 << 20),
        name="late",
    )(place, *feats, *weights[5:], bias, act, w_all)
    keep = pl.pallas_call(
        kept_kernel,
        out_shape=part,
        in_specs=[VMEM, VMEM],
        out_specs=VMEM,
        compiler_params=params,
        cost_estimate=cost(2 * SRC * HID * D_OUT, 2 << 20),
        name="kept",
    )(kept, w_all)
    return give, keep


def norm_kernel(parts_ref, bias_ref, out_ref):
    projected = bias_ref[...]
    for i in range(4):
        projected = projected + parts_ref[i].astype(F32)
    scale = lax.rsqrt(jnp.mean(projected * projected, axis=1, keepdims=True) + 1e-06)
    scaled = (projected * scale).astype(BF16)
    for q in range(4):
        out_ref[q] = scaled[:, q * SHARE : (q + 1) * SHARE]


def norm(parts, bias):
    return pl.pallas_call(
        norm_kernel,
        out_shape=jax.ShapeDtypeStruct((4, 64, SHARE), BF16),
        in_specs=[VMEM, VMEM],
        out_specs=VMEM,
        compiler_params=pltpu.CompilerParams(vmem_limit_bytes=16 << 20),
        name="norm",
    )(parts, bias)


def write_kernel(table_ref, rows_ref, out_ref, target_ref):
    block = table_ref.shape[0]

    @pl.when(pl.program_id(0) == 0)
    def _():
        lane = lax.broadcasted_iota(jnp.int32, (8, META), 1)
        weight = jnp.where(lane == 0, 64.0, jnp.where(lane == 1, 1.0, 0.0)).astype(BF16)
        target_ref[...] = lax.dot_general(
            weight, rows_ref[:, SHARE:], (((1,), (1,)), ((), ())), preferred_element_type=F32
        )

    row = lax.broadcasted_iota(jnp.int32, (block, 1), 0) + (pl.program_id(0) * block + 1)
    here = jnp.where(row.astype(F32) == target_ref[0:1, :], 1.0, 0.0)
    moved = jnp.dot(here.astype(BF16), rows_ref[:, :SHARE], preferred_element_type=F32)
    hit = jnp.max(here, axis=1, keepdims=True) > 0.5
    out_ref[...] = jnp.where(hit, moved, table_ref[...].astype(F32)).astype(BF16)


def write(table, rows):
    block = 512
    spec = pl.BlockSpec((block, SHARE), lambda i: (i, 0))
    return pl.pallas_call(
        write_kernel,
        out_shape=jax.ShapeDtypeStruct(table.shape, BF16),
        grid=(table.shape[0] // block,),
        in_specs=[spec, pl.BlockSpec(rows.shape, lambda i: (0, 0))],
        out_specs=spec,
        scratch_shapes=[pltpu.VMEM((8, rows.shape[0]), F32)],
        compiler_params=pltpu.CompilerParams(vmem_limit_bytes=32 << 20),
        name="write",
    )(table, rows)


def along_x(block, step):
    return lax.ppermute(block, "x", [(i, (i + step) % 4) for i in range(4)])


def swap(block, axis):
    return lax.ppermute(block, axis, [(0, 1), (1, 0)])


def local(features, item_id, w_in, bias_in, w_out, bias_out, item_table):
    index = {axis: lax.axis_index(axis).astype(jnp.int32) for axis in AXES}
    place = jnp.stack([index["x"], index["zl"] * 2 + index["core"], index["yl"], index["core"]])

    w = jnp.concatenate([w_in, w_out], axis=0).reshape(24, 2, HID).transpose(1, 0, 2)
    w = jnp.broadcast_to(w[None], (16, 2, 24, HID)).reshape(32, 24, HID)
    mine = lax.all_to_all(w, PLANE, split_axis=0, concat_axis=0, tiled=True)
    pair = jnp.stack([features, swap(features, "core")])
    mine, pair = lax.optimization_barrier((mine, pair))
    near = swap(pair, "yl")
    la, rb = along_x(mine[:16], 1), along_x(mine[16:], -1)
    lb, ra = along_x(mine[16:], 1), along_x(mine[:16], -1)
    fa, fb = along_x(la, 1), along_x(rb, -1)

    over = swap(pair, "zl")
    feats = (pair, near, over, swap(near, "zl"))

    halves = [each.reshape(2, 4, 2, 24, HID) for each in (la, lb, ra, rb, fa, fb)]
    weights = [mine.reshape(4, 4, 2, 24, HID)] + halves
    bias = lax.dynamic_slice_in_dim(bias_in, index["yl"] * HID, HID).reshape(1, HID)

    give, keep = tower(place, feats, weights, bias)
    chip = (keep.astype(F32) + swap(give, "core").astype(F32)).astype(BF16)
    parts = lax.all_to_all(chip, ("zl", "yl"), split_axis=0, concat_axis=0, tiled=True)
    columns = norm(parts, bias_out.reshape(1, D_OUT))
    columns = lax.all_to_all(columns, TP, split_axis=0, concat_axis=0, tiled=True)
    columns = columns.reshape(SRC, SHARE)

    owner = item_id // OWN_ROWS
    row = item_id - owner * OWN_ROWS + 1
    order = jnp.arange(SRC, dtype=jnp.int32)
    before = (owner[:, None] == owner[None, :]) & (order[None, :] < order[:, None])
    place_of = (owner & 1) * 64 + ((owner >> 1) & 3) * 16 + ((owner >> 3) & 3) * 4 + (owner >> 5)
    slot = place_of * CAP + jnp.sum(before.astype(jnp.int32), axis=1)
    pick = (jnp.arange(OWNERS * CAP, dtype=jnp.int32)[:, None] == slot[None, :]).astype(BF16)
    lane = jnp.arange(META, dtype=jnp.int32)[None, :]
    meta = jnp.where(
        lane == 0,
        (row >> 6)[:, None],
        jnp.where(lane == 1, (row & 63)[:, None], 0),
    ).astype(BF16)
    payload = jnp.concatenate([columns, meta], axis=1)
    packed = jnp.dot(pick, payload, preferred_element_type=F32).astype(BF16)
    arrived = lax.all_to_all(
        packed.reshape(OWNERS, CAP, SHARE + META), ROUTE, split_axis=0, concat_axis=0, tiled=True
    )
    return write(item_table, arrived.reshape(OWNERS * CAP, SHARE + META))


def solution(mesh):
    cut = Mesh(mesh.devices.reshape(SIZES), AXES)
    in_specs = (
        P(SHARD, TP),
        P(SHARD),
        P(SHARD, TP),
        P(TP),
        P(SHARD, TP),
        P(),
        P(SHARD, TP),
    )
    return jax.shard_map(
        local, mesh=cut, in_specs=in_specs, out_specs=P(SHARD, TP), check_vma=False
    )
```

```python
import jax
import jax.numpy as jnp
from jax import lax
from jax.experimental import pallas as pl
from jax.experimental.pallas import tpu as pltpu
from jax.sharding import Mesh, PartitionSpec as P

AXES = ("zh", "x", "yh", "yl", "zl", "core")
SIZES = (4, 4, 4, 2, 2, 2)
SHARD = ("zh", "x", "yh", "yl")
TP = ("zl", "core")
ROUTE = ("yl", "yh", "x", "zh")
PLANE = ("yh", "zh", "yl")

SRC = 256
CAP = 4
OWNERS = 128
OWN_ROWS = 2048
D_OUT = 1024
SHARE = 256
HID = 512
META = 128
BF16 = jnp.bfloat16
F32 = jnp.float32
VMEM = pl.BlockSpec(memory_space=pltpu.VMEM)
SMEM = pl.BlockSpec(memory_space=pltpu.SMEM)


def add_block(x0, tp, offset, first, second, feats, act, w_all):
    xk = lax.rem(x0 + offset, 4)
    col = pl.multiple_of(xk * 128, 128)
    act = list(act)
    for dz in range(2):
        weights = jnp.concatenate(
            [
                half[:, jnp.bitwise_xor(tp, dz * 2 + dc), :, 0:16, :].reshape(64, HID)
                for dc in range(2)
                for half in (first, second)
            ],
            axis=0,
        )
        for dy in range(2):
            columns = jnp.concatenate(
                [feats[dz][dy][dc, :, pl.ds(col, 128)] for dc in range(2)], axis=1
            )
            term = jnp.dot(columns, weights, preferred_element_type=F32)
            act[dy] = term if act[dy] is None else act[dy] + term
    for zh in range(4):
        rows = jnp.concatenate(
            [half[:, zh].astype(F32)[:, :, 16:24, :].reshape(32, HID) for half in (first, second)],
            axis=0,
        )
        row = pl.multiple_of(zh * 256 + xk * 64, 64)
        w_all[pl.ds(row, 64), :] = rows.astype(BF16)
    return act


def tower_kernel(
    place_ref, f0, f1, f2, f3, mine, left, ra, rb, fa, fb, bias_ref, give_ref, kept_ref, w_all, hid
):
    x0, tp, yl, core = (place_ref[i] for i in range(4))
    feats = ((f0, f1), (f2, f3))
    act = [None, None]
    blocks = (
        (0, mine.at[0:2], mine.at[2:4]),
        (3, left.at[0:2], left.at[2:4]),
        (1, ra, rb),
        (2, fa, fb),
    )
    for offset, first, second in blocks:
        act = add_block(x0, tp, offset, first, second, feats, act, w_all)
    for dy in range(2):
        v = act[dy] + bias_ref[...]
        hid[dy] = (v * (1.0 / (1.0 + jnp.exp(-v)))).astype(BF16)

    def chunks(c):
        return [
            hid[dy, pl.ds(pl.multiple_of(zl * 128 + c * 64, 64), 64), :]
            for dy in range(2)
            for zl in range(2)
        ]

    part = lax.dot_general(
        jnp.concatenate(chunks(1 - core), axis=0),
        w_all[...],
        (((1,), (1,)), ((), ())),
        preferred_element_type=F32,
    ).astype(BF16)
    for i, chunk in enumerate(chunks(core)):
        slot = (i % 2) * 2 + jnp.bitwise_xor(yl, i // 2)
        give_ref[slot] = part[i * 64 : (i + 1) * 64]
        kept_ref[pl.ds(pl.multiple_of(slot * 64, 64), 64), :] = chunk


def kept_kernel(kept_ref, w_all, out_ref):
    part = lax.dot_general(
        kept_ref[...], w_all[...], (((1,), (1,)), ((), ())), preferred_element_type=F32
    )
    out_ref[...] = part.astype(BF16).reshape(out_ref.shape)


def cost(flops, moved):
    return pl.CostEstimate(flops=flops, bytes_accessed=moved, transcendentals=0)


def tower(place, feats, weights, bias):
    params = pltpu.CompilerParams(vmem_limit_bytes=48 << 20)
    part = jax.ShapeDtypeStruct((4, 64, D_OUT), BF16)
    w_shape = jax.ShapeDtypeStruct((D_OUT, HID), BF16)
    give, kept, w_all = pl.pallas_call(
        tower_kernel,
        out_shape=(part, jax.ShapeDtypeStruct((SRC, HID), BF16), w_shape),
        in_specs=[SMEM] + [VMEM] * 11,
        out_specs=(VMEM, VMEM, VMEM),
        scratch_shapes=[pltpu.VMEM((2, SRC, HID), BF16)],
        compiler_params=params,
        name="tower",
    )(place, *feats, *weights, bias)
    keep = pl.pallas_call(
        kept_kernel,
        out_shape=part,
        in_specs=[VMEM, VMEM],
        out_specs=VMEM,
        compiler_params=params,
        cost_estimate=cost(2 * SRC * HID * D_OUT, 2 << 20),
        name="kept",
    )(kept, w_all)
    return give, keep


def norm_kernel(parts_ref, bias_ref, out_ref):
    projected = bias_ref[...]
    for i in range(4):
        projected = projected + parts_ref[i].astype(F32)
    scale = lax.rsqrt(jnp.mean(projected * projected, axis=1, keepdims=True) + 1e-06)
    scaled = (projected * scale).astype(BF16)
    for q in range(4):
        out_ref[q] = scaled[:, q * SHARE : (q + 1) * SHARE]


def norm(parts, bias):
    return pl.pallas_call(
        norm_kernel,
        out_shape=jax.ShapeDtypeStruct((4, 64, SHARE), BF16),
        in_specs=[VMEM, VMEM],
        out_specs=VMEM,
        compiler_params=pltpu.CompilerParams(vmem_limit_bytes=16 << 20),
        name="norm",
    )(parts, bias)


def write_kernel(table_ref, rows_ref, out_ref, target_ref):
    block = table_ref.shape[0]

    @pl.when(pl.program_id(0) == 0)
    def _():
        lane = lax.broadcasted_iota(jnp.int32, (8, META), 1)
        weight = jnp.where(lane == 0, 64.0, jnp.where(lane == 1, 1.0, 0.0)).astype(BF16)
        target_ref[...] = lax.dot_general(
            weight, rows_ref[:, SHARE:], (((1,), (1,)), ((), ())), preferred_element_type=F32
        )

    row = lax.broadcasted_iota(jnp.int32, (block, 1), 0) + (pl.program_id(0) * block + 1)
    here = jnp.where(row.astype(F32) == target_ref[0:1, :], 1.0, 0.0)
    moved = jnp.dot(here.astype(BF16), rows_ref[:, :SHARE], preferred_element_type=F32)
    hit = jnp.max(here, axis=1, keepdims=True) > 0.5
    out_ref[...] = jnp.where(hit, moved, table_ref[...].astype(F32)).astype(BF16)


def write(table, rows):
    block = 512
    spec = pl.BlockSpec((block, SHARE), lambda i: (i, 0))
    return pl.pallas_call(
        write_kernel,
        out_shape=jax.ShapeDtypeStruct(table.shape, BF16),
        grid=(table.shape[0] // block,),
        in_specs=[spec, pl.BlockSpec(rows.shape, lambda i: (0, 0))],
        out_specs=spec,
        scratch_shapes=[pltpu.VMEM((8, rows.shape[0]), F32)],
        compiler_params=pltpu.CompilerParams(vmem_limit_bytes=32 << 20),
        name="write",
    )(table, rows)


def along_x(block, step):
    return lax.ppermute(block, "x", [(i, (i + step) % 4) for i in range(4)])


def swap(block, axis):
    return lax.ppermute(block, axis, [(0, 1), (1, 0)])


def local(features, item_id, w_in, bias_in, w_out, bias_out, item_table):
    index = {axis: lax.axis_index(axis).astype(jnp.int32) for axis in AXES}
    place = jnp.stack([index["x"], index["zl"] * 2 + index["core"], index["yl"], index["core"]])

    w = jnp.concatenate([w_in, w_out], axis=0).reshape(24, 2, HID).transpose(1, 0, 2)
    w = jnp.broadcast_to(w[None], (16, 2, 24, HID)).reshape(32, 24, HID)
    mine = lax.all_to_all(w, PLANE, split_axis=0, concat_axis=0, tiled=True)
    pair = jnp.stack([features, swap(features, "core")])
    mine, pair = lax.optimization_barrier((mine, pair))
    near = swap(pair, "yl")
    left = along_x(mine, 1)
    rb, ra = along_x(mine[16:], -1), along_x(mine[:16], -1)
    fa, fb = along_x(left[:16], 1), along_x(rb, -1)

    over = swap(pair, "zl")
    feats = (pair, near, over, swap(near, "zl"))

    weights = [each.reshape(-1, 4, 2, 24, HID) for each in (mine, left, ra, rb, fa, fb)]
    bias = lax.dynamic_slice_in_dim(bias_in, index["yl"] * HID, HID).reshape(1, HID)

    give, keep = tower(place, feats, weights, bias)
    chip = (keep.astype(F32) + swap(give, "core").astype(F32)).astype(BF16)
    parts = lax.all_to_all(chip, ("zl", "yl"), split_axis=0, concat_axis=0, tiled=True)
    columns = norm(parts, bias_out.reshape(1, D_OUT))
    columns = lax.all_to_all(columns, TP, split_axis=0, concat_axis=0, tiled=True)
    columns = columns.reshape(SRC, SHARE)

    owner = item_id // OWN_ROWS
    row = item_id - owner * OWN_ROWS + 1
    order = jnp.arange(SRC, dtype=jnp.int32)
    before = (owner[:, None] == owner[None, :]) & (order[None, :] < order[:, None])
    place_of = (owner & 1) * 64 + ((owner >> 1) & 3) * 16 + ((owner >> 3) & 3) * 4 + (owner >> 5)
    slot = place_of * CAP + jnp.sum(before.astype(jnp.int32), axis=1)
    pick = (jnp.arange(OWNERS * CAP, dtype=jnp.int32)[:, None] == slot[None, :]).astype(BF16)
    lane = jnp.arange(META, dtype=jnp.int32)[None, :]
    meta = jnp.where(
        lane == 0,
        (row >> 6)[:, None],
        jnp.where(lane == 1, (row & 63)[:, None], 0),
    ).astype(BF16)
    payload = jnp.concatenate([columns, meta], axis=1)
    packed = jnp.dot(pick, payload, preferred_element_type=F32).astype(BF16)
    arrived = lax.all_to_all(
        packed.reshape(OWNERS, CAP, SHARE + META), ROUTE, split_axis=0, concat_axis=0, tiled=True
    )
    return write(item_table, arrived.reshape(OWNERS * CAP, SHARE + META))


def solution(mesh):
    cut = Mesh(mesh.devices.reshape(SIZES), AXES)
    in_specs = (
        P(SHARD, TP),
        P(SHARD),
        P(SHARD, TP),
        P(TP),
        P(SHARD, TP),
        P(),
        P(SHARD, TP),
    )
    return jax.shard_map(
        local, mesh=cut, in_specs=in_specs, out_specs=P(SHARD, TP), check_vma=False
    )
```

```python
import jax
import jax.numpy as jnp
from jax import lax
from jax.experimental import pallas as pl
from jax.experimental.pallas import tpu as pltpu
from jax.sharding import Mesh, PartitionSpec as P

AXES = ("zh", "x", "yh", "yl", "zl", "core")
SIZES = (4, 4, 4, 2, 2, 2)
SHARD = ("zh", "x", "yh", "yl")
TP = ("zl", "core")
ROUTE = ("yl", "yh", "x", "zh")
PLANE = ("yh", "zh", "yl")

SRC = 256
CAP = 4
OWNERS = 128
OWN_ROWS = 2048
D_OUT = 1024
SHARE = 256
HID = 512
META = 128
BF16 = jnp.bfloat16
F32 = jnp.float32
VMEM = pl.BlockSpec(memory_space=pltpu.VMEM)
SMEM = pl.BlockSpec(memory_space=pltpu.SMEM)


def add_block(x0, tp, offset, first, second, feats, act, w_all):
    xk = lax.rem(x0 + offset, 4)
    col = pl.multiple_of(xk * 128, 128)
    act = list(act)
    for dz in range(2):
        weights = jnp.concatenate(
            [
                half[:, jnp.bitwise_xor(tp, dz * 2 + dc), :, 0:16, :].reshape(64, HID)
                for dc in range(2)
                for half in (first, second)
            ],
            axis=0,
        )
        for dy in range(2):
            columns = jnp.concatenate(
                [feats[dz][dy][dc, :, pl.ds(col, 128)] for dc in range(2)], axis=1
            )
            term = jnp.dot(columns, weights, preferred_element_type=F32)
            act[dy] = term if act[dy] is None else act[dy] + term
    for zh in range(4):
        rows = jnp.concatenate(
            [half[:, zh].astype(F32)[:, :, 16:24, :].reshape(32, HID) for half in (first, second)],
            axis=0,
        )
        row = pl.multiple_of(zh * 256 + xk * 64, 64)
        w_all[pl.ds(row, 64), :] = rows.astype(BF16)
    return act


def tower_kernel(
    place_ref, f0, f1, f2, f3, mine, la, lb, ra, rb, fa, fb, bias_ref, give_ref, keep_ref, w_all, hid
):
    x0, tp, yl, core = (place_ref[i] for i in range(4))
    feats = ((f0, f1), (f2, f3))
    act = [None, None]
    blocks = ((0, mine.at[0:2], mine.at[2:4]), (3, la, lb), (1, ra, rb), (2, fa, fb))
    for offset, first, second in blocks:
        act = add_block(x0, tp, offset, first, second, feats, act, w_all)
    for dy in range(2):
        v = act[dy] + bias_ref[...]
        hid[dy] = (v * (1.0 / (1.0 + jnp.exp(-v)))).astype(BF16)

    for out_ref, c in ((give_ref, 1 - core), (keep_ref, core)):
        chunks = [
            hid[dy, pl.ds(pl.multiple_of(zl * 128 + c * 64, 64), 64), :]
            for dy in range(2)
            for zl in range(2)
        ]
        part = lax.dot_general(
            jnp.concatenate(chunks, axis=0),
            w_all[...],
            (((1,), (1,)), ((), ())),
            preferred_element_type=F32,
        ).astype(BF16)
        for i in range(4):
            out_ref[(i % 2) * 2 + jnp.bitwise_xor(yl, i // 2)] = part[i * 64 : (i + 1) * 64]


def tower(place, feats, weights, bias):
    part = jax.ShapeDtypeStruct((4, 64, D_OUT), BF16)
    return pl.pallas_call(
        tower_kernel,
        out_shape=(part, part),
        in_specs=[SMEM] + [VMEM] * 12,
        out_specs=(VMEM, VMEM),
        scratch_shapes=[pltpu.VMEM((D_OUT, HID), BF16), pltpu.VMEM((2, SRC, HID), BF16)],
        compiler_params=pltpu.CompilerParams(vmem_limit_bytes=48 << 20),
        name="tower",
    )(place, *feats, *weights, bias)


def norm_kernel(parts_ref, bias_ref, out_ref):
    projected = bias_ref[...]
    for i in range(4):
        projected = projected + parts_ref[i].astype(F32)
    scale = lax.rsqrt(jnp.mean(projected * projected, axis=1, keepdims=True) + 1e-06)
    scaled = (projected * scale).astype(BF16)
    for q in range(4):
        out_ref[q] = scaled[:, q * SHARE : (q + 1) * SHARE]


def norm(parts, bias):
    return pl.pallas_call(
        norm_kernel,
        out_shape=jax.ShapeDtypeStruct((4, 64, SHARE), BF16),
        in_specs=[VMEM, VMEM],
        out_specs=VMEM,
        compiler_params=pltpu.CompilerParams(vmem_limit_bytes=16 << 20),
        name="norm",
    )(parts, bias)


def write_kernel(table_ref, rows_ref, out_ref, target_ref):
    block = table_ref.shape[0]

    @pl.when(pl.program_id(0) == 0)
    def _():
        lane = lax.broadcasted_iota(jnp.int32, (8, META), 1)
        weight = jnp.where(lane == 0, 64.0, jnp.where(lane == 1, 1.0, 0.0)).astype(BF16)
        target_ref[...] = lax.dot_general(
            weight, rows_ref[:, SHARE:], (((1,), (1,)), ((), ())), preferred_element_type=F32
        )

    row = lax.broadcasted_iota(jnp.int32, (block, 1), 0) + (pl.program_id(0) * block + 1)
    here = jnp.where(row.astype(F32) == target_ref[0:1, :], 1.0, 0.0)
    moved = jnp.dot(here.astype(BF16), rows_ref[:, :SHARE], preferred_element_type=F32)
    hit = jnp.max(here, axis=1, keepdims=True) > 0.5
    out_ref[...] = jnp.where(hit, moved, table_ref[...].astype(F32)).astype(BF16)


def write(table, rows):
    block = 512
    spec = pl.BlockSpec((block, SHARE), lambda i: (i, 0))
    return pl.pallas_call(
        write_kernel,
        out_shape=jax.ShapeDtypeStruct(table.shape, BF16),
        grid=(table.shape[0] // block,),
        in_specs=[spec, pl.BlockSpec(rows.shape, lambda i: (0, 0))],
        out_specs=spec,
        scratch_shapes=[pltpu.VMEM((8, rows.shape[0]), F32)],
        compiler_params=pltpu.CompilerParams(vmem_limit_bytes=32 << 20),
        name="write",
    )(table, rows)


def along_x(block, step):
    return lax.ppermute(block, "x", [(i, (i + step) % 4) for i in range(4)])


def swap(block, axis):
    return lax.ppermute(block, axis, [(0, 1), (1, 0)])


def local(features, item_id, w_in, bias_in, w_out, bias_out, item_table):
    index = {axis: lax.axis_index(axis).astype(jnp.int32) for axis in AXES}
    place = jnp.stack([index["x"], index["zl"] * 2 + index["core"], index["yl"], index["core"]])

    w = jnp.concatenate([w_in, w_out], axis=0).reshape(24, 2, HID).transpose(1, 0, 2)
    w = jnp.broadcast_to(w[None], (16, 2, 24, HID)).reshape(32, 24, HID)
    mine = lax.all_to_all(w, PLANE, split_axis=0, concat_axis=0, tiled=True)
    pair = jnp.stack([features, swap(features, "core")])
    mine, pair = lax.optimization_barrier((mine, pair))
    near = swap(pair, "yl")
    left = along_x(mine, 1)
    rb, ra = along_x(mine[16:], -1), along_x(mine[:16], -1)
    la, lb = left[:16], left[16:]
    fa, fb = along_x(la, 1), along_x(rb, -1)

    over = swap(pair, "zl")
    feats = (pair, near, over, swap(near, "zl"))

    weights = [each.reshape(-1, 4, 2, 24, HID) for each in (mine, la, lb, ra, rb, fa, fb)]
    bias = lax.dynamic_slice_in_dim(bias_in, index["yl"] * HID, HID).reshape(1, HID)

    give, keep = tower(place, feats, weights, bias)
    chip = (keep.astype(F32) + swap(give, "core").astype(F32)).astype(BF16)
    parts = lax.all_to_all(chip, ("zl", "yl"), split_axis=0, concat_axis=0, tiled=True)
    columns = norm(parts, bias_out.reshape(1, D_OUT))
    columns = lax.all_to_all(columns, TP, split_axis=0, concat_axis=0, tiled=True)
    columns = columns.reshape(SRC, SHARE)

    owner = item_id // OWN_ROWS
    row = item_id - owner * OWN_ROWS + 1
    order = jnp.arange(SRC, dtype=jnp.int32)
    before = (owner[:, None] == owner[None, :]) & (order[None, :] < order[:, None])
    place_of = (owner & 1) * 64 + ((owner >> 1) & 3) * 16 + ((owner >> 3) & 3) * 4 + (owner >> 5)
    slot = place_of * CAP + jnp.sum(before.astype(jnp.int32), axis=1)
    pick = (jnp.arange(OWNERS * CAP, dtype=jnp.int32)[:, None] == slot[None, :]).astype(BF16)
    lane = jnp.arange(META, dtype=jnp.int32)[None, :]
    meta = jnp.where(
        lane == 0,
        (row >> 6)[:, None],
        jnp.where(lane == 1, (row & 63)[:, None], 0),
    ).astype(BF16)
    payload = jnp.concatenate([columns, meta], axis=1)
    packed = jnp.dot(pick, payload, preferred_element_type=F32).astype(BF16)
    arrived = lax.all_to_all(
        packed.reshape(OWNERS, CAP, SHARE + META), ROUTE, split_axis=0, concat_axis=0, tiled=True
    )
    return write(item_table, arrived.reshape(OWNERS * CAP, SHARE + META))


def solution(mesh):
    cut = Mesh(mesh.devices.reshape(SIZES), AXES)
    in_specs = (
        P(SHARD, TP),
        P(SHARD),
        P(SHARD, TP),
        P(TP),
        P(SHARD, TP),
        P(),
        P(SHARD, TP),
    )
    return jax.shard_map(
        local, mesh=cut, in_specs=in_specs, out_specs=P(SHARD, TP), check_vma=False
    )
```

```python
import jax
import jax.numpy as jnp
from jax import lax
from jax.experimental import pallas as pl
from jax.experimental.pallas import tpu as pltpu
from jax.sharding import Mesh, PartitionSpec as P

AXES = ("zh", "x", "yh", "yl", "zl", "core")
SIZES = (4, 4, 4, 2, 2, 2)
SHARD = ("zh", "x", "yh", "yl")
TP = ("zl", "core")
ROUTE = ("yl", "yh", "x", "zh")
PLANE = ("yh", "zh", "yl")

SRC = 256
CAP = 4
OWNERS = 128
OWN_ROWS = 2048
D_OUT = 1024
SHARE = 256
HID = 512
META = 128
BF16 = jnp.bfloat16
F32 = jnp.float32
VMEM = pl.BlockSpec(memory_space=pltpu.VMEM)
SMEM = pl.BlockSpec(memory_space=pltpu.SMEM)


def add_block(x0, tp, yl, offset, first, second, feats, act, w_all):
    xk = lax.rem(x0 + offset, 4)
    col = pl.multiple_of(xk * 128, 128)
    act = list(act)
    for dz in range(2):
        zl = jnp.bitwise_xor(lax.shift_right_logical(tp, 1), dz)
        weights = jnp.concatenate(
            [
                half[:, jnp.bitwise_xor(tp, dz * 2 + dc), :, 0:16, :].reshape(64, HID)
                for dc in range(2)
                for half in (first, second)
            ],
            axis=0,
        )
        for dy in range(2):
            chip = zl * 2 + jnp.bitwise_xor(yl, dy)
            columns = jnp.concatenate(
                [feats[chip, dc, :, pl.ds(col, 128)] for dc in range(2)], axis=1
            )
            term = jnp.dot(columns, weights, preferred_element_type=F32)
            act[dy] = term if act[dy] is None else act[dy] + term
    for zh in range(4):
        rows = jnp.concatenate(
            [half[:, zh].astype(F32)[:, :, 16:24, :].reshape(32, HID) for half in (first, second)],
            axis=0,
        )
        row = pl.multiple_of(zh * 256 + xk * 64, 64)
        w_all[pl.ds(row, 64), :] = rows.astype(BF16)
    return act


def tower_kernel(
    place_ref, feats, mine, la, lb, ra, rb, fa, fb, bias_ref, give_ref, keep_ref, w_all, hid
):
    x0, tp, yl, core = (place_ref[i] for i in range(4))
    act = [None, None]
    blocks = ((0, mine.at[0:2], mine.at[2:4]), (3, la, lb), (1, ra, rb), (2, fa, fb))
    for offset, first, second in blocks:
        act = add_block(x0, tp, yl, offset, first, second, feats, act, w_all)
    for dy in range(2):
        v = act[dy] + bias_ref[...]
        hid[dy] = (v * (1.0 / (1.0 + jnp.exp(-v)))).astype(BF16)

    for out_ref, c in ((give_ref, 1 - core), (keep_ref, core)):
        chunks = [
            hid[dy, pl.ds(pl.multiple_of(zl * 128 + c * 64, 64), 64), :]
            for dy in range(2)
            for zl in range(2)
        ]
        part = lax.dot_general(
            jnp.concatenate(chunks, axis=0),
            w_all[...],
            (((1,), (1,)), ((), ())),
            preferred_element_type=F32,
        ).astype(BF16)
        for i in range(4):
            out_ref[(i % 2) * 2 + jnp.bitwise_xor(yl, i // 2)] = part[i * 64 : (i + 1) * 64]


def tower(place, feats, weights, bias):
    part = jax.ShapeDtypeStruct((4, 64, D_OUT), BF16)
    return pl.pallas_call(
        tower_kernel,
        out_shape=(part, part),
        in_specs=[SMEM] + [VMEM] * 9,
        out_specs=(VMEM, VMEM),
        scratch_shapes=[pltpu.VMEM((D_OUT, HID), BF16), pltpu.VMEM((2, SRC, HID), BF16)],
        compiler_params=pltpu.CompilerParams(vmem_limit_bytes=48 << 20),
        name="tower",
    )(place, feats, *weights, bias)


def norm_kernel(parts_ref, bias_ref, out_ref):
    projected = bias_ref[...]
    for i in range(4):
        projected = projected + parts_ref[i].astype(F32)
    scale = lax.rsqrt(jnp.mean(projected * projected, axis=1, keepdims=True) + 1e-06)
    scaled = (projected * scale).astype(BF16)
    for q in range(4):
        out_ref[q] = scaled[:, q * SHARE : (q + 1) * SHARE]


def norm(parts, bias):
    return pl.pallas_call(
        norm_kernel,
        out_shape=jax.ShapeDtypeStruct((4, 64, SHARE), BF16),
        in_specs=[VMEM, VMEM],
        out_specs=VMEM,
        compiler_params=pltpu.CompilerParams(vmem_limit_bytes=16 << 20),
        name="norm",
    )(parts, bias)


def write_kernel(table_ref, rows_ref, out_ref, target_ref):
    block = table_ref.shape[0]

    @pl.when(pl.program_id(0) == 0)
    def _():
        lane = lax.broadcasted_iota(jnp.int32, (8, META), 1)
        weight = jnp.where(lane == 0, 64.0, jnp.where(lane == 1, 1.0, 0.0)).astype(BF16)
        target_ref[...] = lax.dot_general(
            weight, rows_ref[:, SHARE:], (((1,), (1,)), ((), ())), preferred_element_type=F32
        )

    row = lax.broadcasted_iota(jnp.int32, (block, 1), 0) + (pl.program_id(0) * block + 1)
    here = jnp.where(row.astype(F32) == target_ref[0:1, :], 1.0, 0.0)
    moved = jnp.dot(here.astype(BF16), rows_ref[:, :SHARE], preferred_element_type=F32)
    hit = jnp.max(here, axis=1, keepdims=True) > 0.5
    out_ref[...] = jnp.where(hit, moved, table_ref[...].astype(F32)).astype(BF16)


def write(table, rows):
    block = 512
    spec = pl.BlockSpec((block, SHARE), lambda i: (i, 0))
    return pl.pallas_call(
        write_kernel,
        out_shape=jax.ShapeDtypeStruct(table.shape, BF16),
        grid=(table.shape[0] // block,),
        in_specs=[spec, pl.BlockSpec(rows.shape, lambda i: (0, 0))],
        out_specs=spec,
        scratch_shapes=[pltpu.VMEM((8, rows.shape[0]), F32)],
        compiler_params=pltpu.CompilerParams(vmem_limit_bytes=32 << 20),
        name="write",
    )(table, rows)


def along_x(block, step):
    return lax.ppermute(block, "x", [(i, (i + step) % 4) for i in range(4)])


def swap(block, axis):
    return lax.ppermute(block, axis, [(0, 1), (1, 0)])


def local(features, item_id, w_in, bias_in, w_out, bias_out, item_table):
    index = {axis: lax.axis_index(axis).astype(jnp.int32) for axis in AXES}
    place = jnp.stack([index["x"], index["zl"] * 2 + index["core"], index["yl"], index["core"]])

    w = jnp.concatenate([w_in, w_out], axis=0).reshape(24, 2, HID).transpose(1, 0, 2)
    w = jnp.broadcast_to(w[None], (16, 2, 24, HID)).reshape(32, 24, HID)
    mine = lax.all_to_all(w, PLANE, split_axis=0, concat_axis=0, tiled=True)
    pair = jnp.stack([features, swap(features, "core")])
    copies = jnp.broadcast_to(pair[None], (4, 2, SRC, 512))
    mine, copies = lax.optimization_barrier((mine, copies))
    left = along_x(mine, 1)
    rb, ra = along_x(mine[16:], -1), along_x(mine[:16], -1)
    la, lb = left[:16], left[16:]
    fa, fb = along_x(la, 1), along_x(rb, -1)

    feats = lax.all_to_all(copies, ("zl", "yl"), split_axis=0, concat_axis=0, tiled=True)
    weights = [each.reshape(-1, 4, 2, 24, HID) for each in (mine, la, lb, ra, rb, fa, fb)]
    bias = lax.dynamic_slice_in_dim(bias_in, index["yl"] * HID, HID).reshape(1, HID)

    give, keep = tower(place, feats, weights, bias)
    chip = (keep.astype(F32) + swap(give, "core").astype(F32)).astype(BF16)
    parts = lax.all_to_all(chip, ("zl", "yl"), split_axis=0, concat_axis=0, tiled=True)
    columns = norm(parts, bias_out.reshape(1, D_OUT))
    columns = lax.all_to_all(columns, TP, split_axis=0, concat_axis=0, tiled=True)
    columns = columns.reshape(SRC, SHARE)

    owner = item_id // OWN_ROWS
    row = item_id - owner * OWN_ROWS + 1
    order = jnp.arange(SRC, dtype=jnp.int32)
    before = (owner[:, None] == owner[None, :]) & (order[None, :] < order[:, None])
    place_of = (owner & 1) * 64 + ((owner >> 1) & 3) * 16 + ((owner >> 3) & 3) * 4 + (owner >> 5)
    slot = place_of * CAP + jnp.sum(before.astype(jnp.int32), axis=1)
    pick = (jnp.arange(OWNERS * CAP, dtype=jnp.int32)[:, None] == slot[None, :]).astype(BF16)
    lane = jnp.arange(META, dtype=jnp.int32)[None, :]
    meta = jnp.where(
        lane == 0,
        (row >> 6)[:, None],
        jnp.where(lane == 1, (row & 63)[:, None], 0),
    ).astype(BF16)
    payload = jnp.concatenate([columns, meta], axis=1)
    packed = jnp.dot(pick, payload, preferred_element_type=F32).astype(BF16)
    arrived = lax.all_to_all(
        packed.reshape(OWNERS, CAP, SHARE + META), ROUTE, split_axis=0, concat_axis=0, tiled=True
    )
    return write(item_table, arrived.reshape(OWNERS * CAP, SHARE + META))


def solution(mesh):
    cut = Mesh(mesh.devices.reshape(SIZES), AXES)
    in_specs = (
        P(SHARD, TP),
        P(SHARD),
        P(SHARD, TP),
        P(TP),
        P(SHARD, TP),
        P(),
        P(SHARD, TP),
    )
    return jax.shard_map(
        local, mesh=cut, in_specs=in_specs, out_specs=P(SHARD, TP), check_vma=False
    )
```

```python
import jax
import jax.numpy as jnp
from jax import lax
from jax.experimental import pallas as pl
from jax.experimental.pallas import tpu as pltpu
from jax.sharding import Mesh, PartitionSpec as P

AXES = ("zh", "x", "yh", "yl", "zl", "core")
SIZES = (4, 4, 4, 2, 2, 2)
SHARD = ("zh", "x", "yh", "yl")
TP = ("zl", "core")
ROUTE = ("yl", "yh", "x", "zh")
PLANE = ("yh", "zh", "yl")

SRC = 256
CAP = 4
OWNERS = 128
OWN_ROWS = 2048
D_OUT = 1024
SHARE = 256
HID = 512
META = 128
BF16 = jnp.bfloat16
F32 = jnp.float32
VMEM = pl.BlockSpec(memory_space=pltpu.VMEM)
SMEM = pl.BlockSpec(memory_space=pltpu.SMEM)


def add_block(x0, tp, yl, offset, first, second, feats, act, w_all):
    xk = lax.rem(x0 + offset, 4)
    col = pl.multiple_of(xk * 128, 128)
    act = list(act)
    for dz in range(2):
        zl = jnp.bitwise_xor(lax.shift_right_logical(tp, 1), dz)
        weights = jnp.concatenate(
            [
                half[:, jnp.bitwise_xor(tp, dz * 2 + dc), :, 0:16, :].reshape(64, HID)
                for dc in range(2)
                for half in (first, second)
            ],
            axis=0,
        )
        for dy in range(2):
            chip = zl * 2 + jnp.bitwise_xor(yl, dy)
            columns = jnp.concatenate(
                [feats[chip, dc, :, pl.ds(col, 128)] for dc in range(2)], axis=1
            )
            term = jnp.dot(columns, weights, preferred_element_type=F32)
            act[dy] = term if act[dy] is None else act[dy] + term
    for zh in range(4):
        rows = jnp.concatenate(
            [half[:, zh].astype(F32)[:, :, 16:24, :].reshape(32, HID) for half in (first, second)],
            axis=0,
        )
        row = pl.multiple_of(zh * 256 + xk * 64, 64)
        w_all[pl.ds(row, 64), :] = rows.astype(BF16)
    return act


def tower_kernel(
    place_ref, feats, mine, la, lb, ra, rb, fa, fb, bias_ref, give_ref, keep_ref, w_all, hid
):
    x0, tp, yl, core = (place_ref[i] for i in range(4))
    act = [None, None]
    blocks = ((0, mine.at[0:2], mine.at[2:4]), (3, la, lb), (1, ra, rb), (2, fa, fb))
    for offset, first, second in blocks:
        act = add_block(x0, tp, yl, offset, first, second, feats, act, w_all)
    for dy in range(2):
        v = act[dy] + bias_ref[...]
        hid[dy] = (v * (1.0 / (1.0 + jnp.exp(-v)))).astype(BF16)

    for out_ref, c in ((give_ref, 1 - core), (keep_ref, core)):
        chunks = [
            hid[dy, pl.ds(pl.multiple_of(zl * 128 + c * 64, 64), 64), :]
            for dy in range(2)
            for zl in range(2)
        ]
        part = lax.dot_general(
            jnp.concatenate(chunks, axis=0),
            w_all[...],
            (((1,), (1,)), ((), ())),
            preferred_element_type=F32,
        ).astype(BF16)
        for i in range(4):
            out_ref[(i % 2) * 2 + jnp.bitwise_xor(yl, i // 2)] = part[i * 64 : (i + 1) * 64]


def tower(place, feats, weights, bias):
    part = jax.ShapeDtypeStruct((4, 64, D_OUT), BF16)
    return pl.pallas_call(
        tower_kernel,
        out_shape=(part, part),
        in_specs=[SMEM] + [VMEM] * 9,
        out_specs=(VMEM, VMEM),
        scratch_shapes=[pltpu.VMEM((D_OUT, HID), BF16), pltpu.VMEM((2, SRC, HID), BF16)],
        compiler_params=pltpu.CompilerParams(vmem_limit_bytes=48 << 20),
        name="tower",
    )(place, feats, *weights, bias)


def norm_kernel(parts_ref, bias_ref, out_ref):
    projected = bias_ref[...]
    for i in range(4):
        projected = projected + parts_ref[i].astype(F32)
    scale = lax.rsqrt(jnp.mean(projected * projected, axis=1, keepdims=True) + 1e-06)
    scaled = (projected * scale).astype(BF16)
    for q in range(4):
        out_ref[q] = scaled[:, q * SHARE : (q + 1) * SHARE]


def norm(parts, bias):
    return pl.pallas_call(
        norm_kernel,
        out_shape=jax.ShapeDtypeStruct((4, 64, SHARE), BF16),
        in_specs=[VMEM, VMEM],
        out_specs=VMEM,
        compiler_params=pltpu.CompilerParams(vmem_limit_bytes=16 << 20),
        name="norm",
    )(parts, bias)


def write_kernel(table_ref, rows_ref, out_ref, target_ref):
    block = table_ref.shape[0]

    @pl.when(pl.program_id(0) == 0)
    def _():
        lane = lax.broadcasted_iota(jnp.int32, (8, META), 1)
        weight = jnp.where(lane == 0, 64.0, jnp.where(lane == 1, 1.0, 0.0)).astype(BF16)
        target_ref[...] = lax.dot_general(
            weight, rows_ref[:, SHARE:], (((1,), (1,)), ((), ())), preferred_element_type=F32
        )

    row = lax.broadcasted_iota(jnp.int32, (block, 1), 0) + (pl.program_id(0) * block + 1)
    here = jnp.where(row.astype(F32) == target_ref[0:1, :], 1.0, 0.0)
    moved = jnp.dot(here.astype(BF16), rows_ref[:, :SHARE], preferred_element_type=F32)
    hit = jnp.max(here, axis=1, keepdims=True) > 0.5
    out_ref[...] = jnp.where(hit, moved, table_ref[...].astype(F32)).astype(BF16)


def write(table, rows):
    block = 512
    spec = pl.BlockSpec((block, SHARE), lambda i: (i, 0))
    return pl.pallas_call(
        write_kernel,
        out_shape=jax.ShapeDtypeStruct(table.shape, BF16),
        grid=(table.shape[0] // block,),
        in_specs=[spec, pl.BlockSpec(rows.shape, lambda i: (0, 0))],
        out_specs=spec,
        scratch_shapes=[pltpu.VMEM((8, rows.shape[0]), F32)],
        compiler_params=pltpu.CompilerParams(vmem_limit_bytes=32 << 20),
        name="write",
    )(table, rows)


def along_x(block, step):
    return lax.ppermute(block, "x", [(i, (i + step) % 4) for i in range(4)])


def swap(block, axis):
    return lax.ppermute(block, axis, [(0, 1), (1, 0)])


def local(features, item_id, w_in, bias_in, w_out, bias_out, item_table):
    index = {axis: lax.axis_index(axis).astype(jnp.int32) for axis in AXES}
    place = jnp.stack([index["x"], index["zl"] * 2 + index["core"], index["yl"], index["core"]])

    w = jnp.concatenate([w_in, w_out], axis=0).reshape(24, 2, HID).transpose(1, 0, 2)
    w = jnp.broadcast_to(w[None], (16, 2, 24, HID)).reshape(32, 24, HID)
    mine = lax.all_to_all(w, PLANE, split_axis=0, concat_axis=0, tiled=True)
    pair = jnp.stack([features, swap(features, "core")])
    copies = jnp.broadcast_to(pair[None], (4, 2, SRC, 512))
    mine, copies = lax.optimization_barrier((mine, copies))
    la, rb = along_x(mine[:16], 1), along_x(mine[16:], -1)
    lb, ra = along_x(mine[16:], 1), along_x(mine[:16], -1)
    fa, fb = along_x(la, 1), along_x(rb, -1)

    feats = lax.all_to_all(copies, ("zl", "yl"), split_axis=0, concat_axis=0, tiled=True)
    weights = [each.reshape(-1, 4, 2, 24, HID) for each in (mine, la, lb, ra, rb, fa, fb)]
    bias = lax.dynamic_slice_in_dim(bias_in, index["yl"] * HID, HID).reshape(1, HID)

    give, keep = tower(place, feats, weights, bias)
    chip = (keep.astype(F32) + swap(give, "core").astype(F32)).astype(BF16)
    parts = lax.all_to_all(chip, ("zl", "yl"), split_axis=0, concat_axis=0, tiled=True)
    columns = norm(parts, bias_out.reshape(1, D_OUT))
    columns = lax.all_to_all(columns, TP, split_axis=0, concat_axis=0, tiled=True)
    columns = columns.reshape(SRC, SHARE)

    owner = item_id // OWN_ROWS
    row = item_id - owner * OWN_ROWS + 1
    order = jnp.arange(SRC, dtype=jnp.int32)
    before = (owner[:, None] == owner[None, :]) & (order[None, :] < order[:, None])
    place_of = (owner & 1) * 64 + ((owner >> 1) & 3) * 16 + ((owner >> 3) & 3) * 4 + (owner >> 5)
    slot = place_of * CAP + jnp.sum(before.astype(jnp.int32), axis=1)
    pick = (jnp.arange(OWNERS * CAP, dtype=jnp.int32)[:, None] == slot[None, :]).astype(BF16)
    lane = jnp.arange(META, dtype=jnp.int32)[None, :]
    meta = jnp.where(
        lane == 0,
        (row >> 6)[:, None],
        jnp.where(lane == 1, (row & 63)[:, None], 0),
    ).astype(BF16)
    payload = jnp.concatenate([columns, meta], axis=1)
    packed = jnp.dot(pick, payload, preferred_element_type=F32).astype(BF16)
    arrived = lax.all_to_all(
        packed.reshape(OWNERS, CAP, SHARE + META), ROUTE, split_axis=0, concat_axis=0, tiled=True
    )
    return write(item_table, arrived.reshape(OWNERS * CAP, SHARE + META))


def solution(mesh):
    cut = Mesh(mesh.devices.reshape(SIZES), AXES)
    in_specs = (
        P(SHARD, TP),
        P(SHARD),
        P(SHARD, TP),
        P(TP),
        P(SHARD, TP),
        P(),
        P(SHARD, TP),
    )
    return jax.shard_map(
        local, mesh=cut, in_specs=in_specs, out_specs=P(SHARD, TP), check_vma=False
    )
```

```python
import jax
import jax.numpy as jnp
from jax import lax
from jax.experimental import pallas as pl
from jax.experimental.pallas import tpu as pltpu
from jax.sharding import Mesh, PartitionSpec as P

AXES = ("zh", "x", "yh", "yl", "zl", "core")
SIZES = (4, 4, 4, 2, 2, 2)
SHARD = ("zh", "x", "yh", "yl")
TP = ("zl", "core")
ROUTE = ("yl", "yh", "x", "zh")
PLANE = ("yh", "zh", "yl")

SRC = 256
CAP = 4
OWNERS = 128
OWN_ROWS = 2048
D_OUT = 1024
SHARE = 256
HID = 512
META = 128
BF16 = jnp.bfloat16
F32 = jnp.float32
VMEM = pl.BlockSpec(memory_space=pltpu.VMEM)
SMEM = pl.BlockSpec(memory_space=pltpu.SMEM)


def add_block(x0, tp, offset, first, second, feats, act, w_all):
    xk = lax.rem(x0 + offset, 4)
    col = pl.multiple_of(xk * 128, 128)
    act = list(act)
    for dz in range(2):
        weights = jnp.concatenate(
            [
                half[:, jnp.bitwise_xor(tp, dz * 2 + dc), :, 0:16, :].reshape(64, HID)
                for dc in range(2)
                for half in (first, second)
            ],
            axis=0,
        )
        for dy in range(2):
            columns = jnp.concatenate(
                [feats[dz][dy][dc, :, pl.ds(col, 128)] for dc in range(2)], axis=1
            )
            term = jnp.dot(columns, weights, preferred_element_type=F32)
            act[dy] = term if act[dy] is None else act[dy] + term
    for zh in range(4):
        rows = jnp.concatenate(
            [half[:, zh].astype(F32)[:, :, 16:24, :].reshape(32, HID) for half in (first, second)],
            axis=0,
        )
        row = pl.multiple_of(zh * 256 + xk * 64, 64)
        w_all[pl.ds(row, 64), :] = rows.astype(BF16)
    return act


def tower_kernel(
    place_ref, f0, f1, f2, f3, mine, la, lb, ra, rb, fa, fb, bias_ref, give_ref, keep_ref, w_all, hid
):
    x0, tp, yl, core = (place_ref[i] for i in range(4))
    feats = ((f0, f1), (f2, f3))
    act = [None, None]
    blocks = ((0, mine.at[0:2], mine.at[2:4]), (3, la, lb), (1, ra, rb), (2, fa, fb))
    for offset, first, second in blocks:
        act = add_block(x0, tp, offset, first, second, feats, act, w_all)
    for dy in range(2):
        v = act[dy] + bias_ref[...]
        hid[dy] = (v * (1.0 / (1.0 + jnp.exp(-v)))).astype(BF16)

    for out_ref, c in ((give_ref, 1 - core), (keep_ref, core)):
        chunks = [
            hid[dy, pl.ds(pl.multiple_of(zl * 128 + c * 64, 64), 64), :]
            for dy in range(2)
            for zl in range(2)
        ]
        part = lax.dot_general(
            jnp.concatenate(chunks, axis=0),
            w_all[...],
            (((1,), (1,)), ((), ())),
            preferred_element_type=F32,
        ).astype(BF16)
        for i in range(4):
            out_ref[(i % 2) * 2 + jnp.bitwise_xor(yl, i // 2)] = part[i * 64 : (i + 1) * 64]


def tower(place, feats, weights, bias):
    part = jax.ShapeDtypeStruct((4, 64, D_OUT), BF16)
    return pl.pallas_call(
        tower_kernel,
        out_shape=(part, part),
        in_specs=[SMEM] + [VMEM] * 12,
        out_specs=(VMEM, VMEM),
        scratch_shapes=[pltpu.VMEM((D_OUT, HID), BF16), pltpu.VMEM((2, SRC, HID), BF16)],
        compiler_params=pltpu.CompilerParams(vmem_limit_bytes=48 << 20),
        name="tower",
    )(place, *feats, *weights, bias)


def norm_kernel(parts_ref, bias_ref, out_ref):
    projected = bias_ref[...]
    for i in range(4):
        projected = projected + parts_ref[i].astype(F32)
    scale = lax.rsqrt(jnp.mean(projected * projected, axis=1, keepdims=True) + 1e-06)
    scaled = (projected * scale).astype(BF16)
    for q in range(4):
        out_ref[q] = scaled[:, q * SHARE : (q + 1) * SHARE]


def norm(parts, bias):
    return pl.pallas_call(
        norm_kernel,
        out_shape=jax.ShapeDtypeStruct((4, 64, SHARE), BF16),
        in_specs=[VMEM, VMEM],
        out_specs=VMEM,
        compiler_params=pltpu.CompilerParams(vmem_limit_bytes=16 << 20),
        name="norm",
    )(parts, bias)


def write_kernel(table_ref, rows_ref, out_ref, target_ref):
    block = table_ref.shape[0]

    @pl.when(pl.program_id(0) == 0)
    def _():
        lane = lax.broadcasted_iota(jnp.int32, (8, META), 1)
        weight = jnp.where(lane == 0, 64.0, jnp.where(lane == 1, 1.0, 0.0)).astype(BF16)
        target_ref[...] = lax.dot_general(
            weight, rows_ref[:, SHARE:], (((1,), (1,)), ((), ())), preferred_element_type=F32
        )

    row = lax.broadcasted_iota(jnp.int32, (block, 1), 0) + (pl.program_id(0) * block + 1)
    here = jnp.where(row.astype(F32) == target_ref[0:1, :], 1.0, 0.0)
    moved = jnp.dot(here.astype(BF16), rows_ref[:, :SHARE], preferred_element_type=F32)
    hit = jnp.max(here, axis=1, keepdims=True) > 0.5
    out_ref[...] = jnp.where(hit, moved, table_ref[...].astype(F32)).astype(BF16)


def write(table, rows):
    block = 1024
    spec = pl.BlockSpec((block, SHARE), lambda i: (i, 0))
    return pl.pallas_call(
        write_kernel,
        out_shape=jax.ShapeDtypeStruct(table.shape, BF16),
        grid=(table.shape[0] // block,),
        in_specs=[spec, pl.BlockSpec(rows.shape, lambda i: (0, 0))],
        out_specs=spec,
        scratch_shapes=[pltpu.VMEM((8, rows.shape[0]), F32)],
        compiler_params=pltpu.CompilerParams(vmem_limit_bytes=32 << 20),
        name="write",
    )(table, rows)


def along_x(block, step):
    return lax.ppermute(block, "x", [(i, (i + step) % 4) for i in range(4)])


def swap(block, axis):
    return lax.ppermute(block, axis, [(0, 1), (1, 0)])


def local(features, item_id, w_in, bias_in, w_out, bias_out, item_table):
    index = {axis: lax.axis_index(axis).astype(jnp.int32) for axis in AXES}
    place = jnp.stack([index["x"], index["zl"] * 2 + index["core"], index["yl"], index["core"]])

    w = jnp.concatenate([w_in, w_out], axis=0).reshape(24, 2, HID).transpose(1, 0, 2)
    w = jnp.broadcast_to(w[None], (16, 2, 24, HID)).reshape(32, 24, HID)
    mine = lax.all_to_all(w, PLANE, split_axis=0, concat_axis=0, tiled=True)
    pair = jnp.stack([features, swap(features, "core")])
    mine, pair = lax.optimization_barrier((mine, pair))
    near = swap(pair, "yl")
    left = along_x(mine, 1)
    rb, ra = along_x(mine[16:], -1), along_x(mine[:16], -1)
    la, lb = left[:16], left[16:]
    fa, fb = along_x(la, 1), along_x(rb, -1)

    over = swap(pair, "zl")
    feats = (pair, near, over, swap(near, "zl"))

    weights = [each.reshape(-1, 4, 2, 24, HID) for each in (mine, la, lb, ra, rb, fa, fb)]
    bias = lax.dynamic_slice_in_dim(bias_in, index["yl"] * HID, HID).reshape(1, HID)

    give, keep = tower(place, feats, weights, bias)
    chip = (keep.astype(F32) + swap(give, "core").astype(F32)).astype(BF16)
    parts = lax.all_to_all(chip, ("zl", "yl"), split_axis=0, concat_axis=0, tiled=True)
    columns = norm(parts, bias_out.reshape(1, D_OUT))
    columns = lax.all_to_all(columns, TP, split_axis=0, concat_axis=0, tiled=True)
    columns = columns.reshape(SRC, SHARE)

    owner = item_id // OWN_ROWS
    row = item_id - owner * OWN_ROWS + 1
    order = jnp.arange(SRC, dtype=jnp.int32)
    before = (owner[:, None] == owner[None, :]) & (order[None, :] < order[:, None])
    place_of = (owner & 1) * 64 + ((owner >> 1) & 3) * 16 + ((owner >> 3) & 3) * 4 + (owner >> 5)
    slot = place_of * CAP + jnp.sum(before.astype(jnp.int32), axis=1)
    pick = (jnp.arange(OWNERS * CAP, dtype=jnp.int32)[:, None] == slot[None, :]).astype(BF16)
    lane = jnp.arange(META, dtype=jnp.int32)[None, :]
    meta = jnp.where(
        lane == 0,
        (row >> 6)[:, None],
        jnp.where(lane == 1, (row & 63)[:, None], 0),
    ).astype(BF16)
    payload = jnp.concatenate([columns, meta], axis=1)
    packed = jnp.dot(pick, payload, preferred_element_type=F32).astype(BF16)
    arrived = lax.all_to_all(
        packed.reshape(OWNERS, CAP, SHARE + META), ROUTE, split_axis=0, concat_axis=0, tiled=True
    )
    return write(item_table, arrived.reshape(OWNERS * CAP, SHARE + META))


def solution(mesh):
    cut = Mesh(mesh.devices.reshape(SIZES), AXES)
    in_specs = (
        P(SHARD, TP),
        P(SHARD),
        P(SHARD, TP),
        P(TP),
        P(SHARD, TP),
        P(),
        P(SHARD, TP),
    )
    return jax.shard_map(
        local, mesh=cut, in_specs=in_specs, out_specs=P(SHARD, TP), check_vma=False
    )
```
